32 devices in a mesh: groups: 2 (over y), patch: 4 (over z), tensor: 4 (over x, core).
Axes of the slice: x: 2, y: 2, z: 4, core: 2. Of those that a mesh axis runs over, the one named last changes fastest.
Arguments:
- hidden_in: bfloat16 [2048, 5120], P(('groups', 'patch'), 'tensor'), parts along dimension 0, may hold values from -10.5 to 10.5
- w_query: bfloat16 [5120, 3072], P('patch', 'tensor'), may hold values from -0.08385255 to 0.08385255
- w_key: bfloat16 [5120, 3072], P('patch', 'tensor'), may hold values from -0.08385255 to 0.08385255
- w_value: bfloat16 [5120, 3072], P('patch', 'tensor'), may hold values from -0.078125 to 0.078125
- w_out: bfloat16 [3072, 5120], P('tensor'), may hold values from -6 to 6
- stale_kv: bfloat16 [2, 2048, 3072], P(None, 'groups', 'tensor'), parts along dimension 1, may hold values from -6 to 6
Outputs:
- attended: bfloat16 [2048, 5120], P(('groups', 'patch'), 'tensor'), parts along dimension 0
- refreshed: bfloat16 [2, 2048, 3072], P(None, 'groups', 'tensor'), parts along dimension 1
The draws below stay inside these ranges and needn't reach their ends.
There are 2 independent parts, one for each index of `groups`. The reference program is written for one: setup_inputs(seed, part) draws one part's arguments, and reference() takes and returns one part's arrays. A program takes and returns all parts, laid end to end along the dimension named above; an argument that names none is the same for every part. Nothing has to cross between parts.
All inputs are finite; a program needn't handle non-finite values.
Results may differ from the reference program's by a relative error of at most 0.0073.
Values may be sent and summed in bfloat16 or wider, within the bound.
No kernel may reach another device: no remote copies, remote signals or barrier semaphores. Data moves between devices by JAX's collectives and lax.ppermute only.
A program may use at most 128 MiB of HBM per device.

```python
import jax
import jax.numpy as jnp
from jax import lax

D = 5120
HEADS = 24
HEAD_DIM = 128
T_DEV = 256
TOKENS = 1024


def shared_rows(key):
    return jnp.clip(jax.random.normal(key, (D, HEADS * HEAD_DIM), jnp.float32), -6.0, 6.0)


def draw_hidden_in(key, part):
    key = jax.random.fold_in(key, 11)
    first = jax.random.fold_in(key, 0)
    return jnp.clip(jax.random.normal(first, (TOKENS, D), jnp.float32), -4.0, 4.0).astype(jnp.bfloat16)


def draw_w_query(key, part):
    base = shared_rows(key)
    return (base / D ** 0.5).astype(jnp.bfloat16)


def draw_w_key(key, part):
    key = jax.random.fold_in(key, 5)
    own = jnp.clip(jax.random.normal(key, (D, HEADS * HEAD_DIM), jnp.float32), -6.0, 6.0)
    return (own / D ** 0.5).astype(jnp.bfloat16)


def levels(key, extent, pieces, least, high):
    loudness = 1.0
    for dim, shards_of in pieces:
        steps = jax.random.uniform(jax.random.fold_in(jax.random.fold_in(key, 6), dim), (shards_of,), jnp.float32, least / len(pieces), high / len(pieces))
        loudness = loudness * jnp.repeat(jnp.exp(steps), extent[dim] // shards_of).reshape((-1,) + (1,) * (len(extent) - 1 - dim))
    return loudness


def scatter_about(key, dims, width, reach, cuts=(), held_as=jnp.bfloat16):
    values = jax.random.normal(key, dims, jnp.float32) * width
    if len(cuts) > 0:
        values = levels(key, dims, cuts, -0.22, 0.18) * values
    return jnp.clip(values, min=-reach, max=reach).astype(held_as)


def setup_inputs(seed: int = 0, part: int = 0) -> dict:
    arg_keys = jax.random.split(jax.random.key(seed), 7)
    part_splits = jax.random.split(jax.random.fold_in(arg_keys[6], part), 7)
    hidden_in = draw_hidden_in(jax.random.fold_in(jax.random.fold_in(arg_keys[6], part), 71), part)
    w_query = draw_w_query(jax.random.fold_in(arg_keys[6], 71), part)
    w_key = draw_w_key(jax.random.fold_in(arg_keys[6], 71), part)
    w_value = scatter_about(arg_keys[3], (D, HEADS * HEAD_DIM), D ** -0.5, 0.078125, ((0, 4), (1, 4)))
    w_out = scatter_about(arg_keys[4], (HEADS * HEAD_DIM, D), 1.0, 6.0, ((0, 4),))
    stale_kv = scatter_about(part_splits[5], (2, TOKENS, HEADS * HEAD_DIM), 1.0, 6.0, ((2, 4),))
    return {"hidden_in": hidden_in, "w_query": w_query, "w_key": w_key, "w_value": w_value, "w_out": w_out, "stale_kv": stale_kv}


def one_head(operands):
    query_h, keys_old, values_old, keys_new, values_new = operands
    scale = 1.0 / (HEAD_DIM ** 0.5)
    rows = jnp.arange(TOKENS, dtype=jnp.int32) // T_DEV
    same = rows[:, None] == rows[None, :]
    scores_old = jnp.dot(query_h, keys_old.T, preferred_element_type=jnp.float32) * scale
    scores_new = jnp.dot(query_h, keys_new.T, preferred_element_type=jnp.float32) * scale
    scores = jnp.where(same, scores_new, scores_old)
    top = jnp.max(scores, axis=-1, keepdims=True)
    expo = jnp.exp(scores - top)
    total = jnp.sum(expo, axis=-1, keepdims=True)
    weights = expo.astype(jnp.bfloat16)
    zero = jnp.zeros_like(weights)
    mixed = jnp.dot(jnp.where(same, zero, weights), values_old, preferred_element_type=jnp.float32)
    mixed = mixed + jnp.dot(jnp.where(same, weights, zero), values_new, preferred_element_type=jnp.float32)
    return (mixed / total).astype(jnp.bfloat16)


def split_heads(matrix):
    return matrix.reshape(TOKENS, HEADS, HEAD_DIM).transpose(1, 0, 2)


def reference(hidden_in, w_query, w_key, w_value, w_out, stale_kv):
    query = jnp.dot(hidden_in, w_query, preferred_element_type=jnp.float32).astype(jnp.bfloat16)
    key_fresh = jnp.dot(hidden_in, w_key, preferred_element_type=jnp.float32).astype(jnp.bfloat16)
    value_fresh = jnp.dot(hidden_in, w_value, preferred_element_type=jnp.float32).astype(jnp.bfloat16)
    fresh = jnp.stack([key_fresh, value_fresh]).astype(jnp.float32)
    delta = (fresh - stale_kv.astype(jnp.float32)).astype(jnp.bfloat16)
    refreshed = (stale_kv.astype(jnp.float32) + delta.astype(jnp.float32)).astype(jnp.bfloat16)
    heads_out = lax.map(one_head, (split_heads(query), split_heads(stale_kv[0]), split_heads(stale_kv[1]), split_heads(refreshed[0]), split_heads(refreshed[1])))
    heads_out = heads_out.transpose(1, 0, 2).reshape(TOKENS, HEADS * HEAD_DIM)
    attended = jnp.dot(heads_out, w_out, preferred_element_type=jnp.float32).astype(jnp.bfloat16)
    return (attended, refreshed)
```

```python
import jax
import jax.numpy as jnp
from jax import lax
from jax.sharding import PartitionSpec as P

HEAD_DIM = 128
F32 = jnp.float32
BF16 = jnp.bfloat16


def spread_features(hidden, patches, ranks):
    if patches == ranks and ranks % 2 == 0:
        half = ranks // 2
        place = [(s % half) * 2 + s // half for s in range(patches)]
        pairs = [(s * ranks + t, t * ranks + place[s]) for s in range(patches) for t in range(ranks)]
        block = lax.ppermute(hidden, ("patch", "tensor"), pairs)
        return lax.all_gather(block, "tensor", axis=0, tiled=True), lambda s: (s % half) * 2 + s // half
    features = lax.all_gather(hidden, "tensor", axis=1, tiled=True)
    return lax.all_to_all(features, "patch", split_axis=1, concat_axis=0, tiled=True), lambda s: s


def sum_own_slab(parts, rows, place, patches):
    me = lax.axis_index("patch")

    def mine(slab):
        slab = jnp.clip(slab, 0, patches - 1)
        return lax.dynamic_slice_in_dim(parts, place(slab) * rows, rows, 0)

    up = down = None
    for step in range(1, patches):
        send_up = mine(patches - step + me)
        send_down = mine(step - patches + me)
        if step > 1:
            send_up = send_up + up.astype(F32)
            send_down = send_down + down.astype(F32)
        up = lax.ppermute(send_up.astype(BF16), "patch", [(i, i + 1) for i in range(step)])
        down = lax.ppermute(
            send_down.astype(BF16), "patch", [(patches - 1 - i, patches - 2 - i) for i in range(step)]
        )
    total = mine(me)
    if patches > 1:
        total = total + (up.astype(F32) + down.astype(F32))
    return total


def sum_columns(heads_out, w_out, ranks):
    rank = lax.axis_index("tensor")
    core, chip, chips = rank % 2, rank // 2, ranks // 2
    depth = w_out.shape[0]
    width = w_out.shape[1] // ranks
    by_core = w_out.reshape(depth, chips, 2, width)

    def columns(which):
        picked = lax.dynamic_index_in_dim(by_core, which, 2, keepdims=False)
        return jnp.dot(heads_out, picked.reshape(depth, chips * width), preferred_element_type=F32)

    swap = [(r, r ^ 1) for r in range(ranks)]
    other = lax.ppermute(columns(1 - core).astype(BF16), "tensor", swap)
    both = columns(core) + other.astype(F32)
    if chips == 1:
        return both.astype(BF16)
    both = both.reshape(-1, chips, width)
    total = None
    for hop in range(1, chips):
        target = (chip + hop) % chips
        block = lax.dynamic_index_in_dim(both, target, 1, keepdims=False)
        pairs = [(r, (r + 2 * hop) % ranks) for r in range(ranks)]
        got = lax.ppermute(block.astype(BF16), "tensor", pairs).astype(F32)
        total = got if total is None else total + got
    total = total + lax.dynamic_index_in_dim(both, chip, 1, keepdims=False)
    return total.astype(BF16)


def make_shards(patches, ranks):
    def shards(hidden_in, w_query, w_key, w_value, w_out, stale_kv):
        rows = hidden_in.shape[0]
        width = w_query.shape[1]
        heads = width // HEAD_DIM
        me = lax.axis_index("patch")
        features, place = spread_features(hidden_in, patches, ranks)

        def project(weight):
            parts = jnp.dot(features, weight, preferred_element_type=F32)
            return sum_own_slab(parts, rows, place, patches).astype(BF16)

        own_stale = lax.dynamic_slice_in_dim(stale_kv, me * rows, rows, 1).astype(F32)

        def refresh(fresh, stale):
            delta = (fresh.astype(F32) - stale).astype(BF16)
            return (stale + delta.astype(F32)).astype(BF16)

        key_new = refresh(project(w_key), own_stale[0])
        query = project(w_query)
        value_new = refresh(project(w_value), own_stale[1])
        keys_all = lax.all_gather(key_new, "patch", axis=0, tiled=True)
        values_all = lax.all_gather(value_new, "patch", axis=0, tiled=True)
        refreshed = jnp.stack([keys_all, values_all])

        def split(matrix):
            return matrix.reshape(-1, heads, HEAD_DIM)

        scale = 1.0 / HEAD_DIM**0.5
        query_h = split(query)

        def score(keys):
            return jnp.einsum("thd,shd->hts", query_h, split(keys), preferred_element_type=F32) * scale

        slab_of = jnp.arange(stale_kv.shape[1], dtype=jnp.int32) // rows
        old = jnp.where(slab_of[None, None, :] == me, -jnp.inf, score(stale_kv[0]))
        new = score(key_new)
        top = jnp.maximum(jnp.max(old, -1, keepdims=True), jnp.max(new, -1, keepdims=True))
        old, new = jnp.exp(old - top), jnp.exp(new - top)
        total = jnp.sum(old, -1) + jnp.sum(new, -1)

        def mix(weights, values):
            return jnp.einsum(
                "hts,shd->thd", weights.astype(BF16), split(values), preferred_element_type=F32
            )

        mixed = mix(old, stale_kv[1]) + mix(new, value_new)
        mixed = mixed / jnp.transpose(total)[:, :, None]
        heads_out = mixed.astype(BF16).reshape(rows, width)
        return (sum_columns(heads_out, w_out, ranks), refreshed)

    return shards


def solution(mesh):
    in_specs = (
        P(("groups", "patch"), "tensor"),
        P("patch", "tensor"),
        P("patch", "tensor"),
        P("patch", "tensor"),
        P("tensor", None),
        P(None, "groups", "tensor"),
    )
    out_specs = (P(("groups", "patch"), "tensor"), P(None, "groups", "tensor"))
    return jax.shard_map(
        make_shards(mesh.shape["patch"], mesh.shape["tensor"]),
        mesh=mesh,
        in_specs=in_specs,
        out_specs=out_specs,
        check_vma=False,
    )
```

```python
import functools

import jax
import jax.numpy as jnp
from jax import lax
from jax.experimental import pallas as pl
from jax.experimental.pallas import tpu as pltpu
from jax.sharding import PartitionSpec as P

HEAD_DIM = 128
F32 = jnp.float32
BF16 = jnp.bfloat16
F16 = jnp.float16
LIFT = 8.0


def spread_features(hidden, patches, ranks):
    if not (patches == ranks == 4):
        features = lax.all_gather(hidden, "tensor", axis=1, tiled=True)
        features = lax.all_to_all(features, "patch", split_axis=1, concat_axis=0, tiled=True)
        return features, lambda s: s
    both = ("patch", "tensor")
    rank = lax.axis_index("tensor")
    core, chip = rank % 2, rank // 2
    half = hidden.shape[0] // 2
    straight, crossing = hidden[:half], hidden[half:]
    across = [(r, r ^ 2) for r in range(ranks)]
    crossing = lax.ppermute(crossing, "tensor", across)

    def along(block, flip, pair):
        pairs = []
        for s in (2 * pair, 2 * pair + 1):
            for r in range(ranks):
                pairs.append((s * ranks + r, (r ^ flip) * ranks + (r // 2) * 2 + s % 2))
        return lax.ppermute(block, both, pairs)

    first = [along(straight, 0, pair) for pair in range(2)]
    second = [along(crossing, 2, pair) for pair in range(2)]
    is_straight = lax.axis_index("patch") // 2 == chip
    held = jnp.stack([jnp.where(is_straight, first[i], second[i]) for i in range(2)])
    other = lax.ppermute(held, "tensor", across)
    low = jnp.where(is_straight, held, other)
    high = jnp.where(is_straight, other, held)
    mine = jnp.concatenate([low, high], axis=1)
    theirs = lax.ppermute(mine, "tensor", [(r, r ^ 1) for r in range(ranks)])
    features = jnp.concatenate([mine, theirs]).reshape(4 * hidden.shape[0], -1)
    return features, lambda s: ((s % 2) ^ core) * 2 + s // 2


def sum_own_slab(parts, rows, place, patches, after=None):
    me = lax.axis_index("patch")

    def mine(slab):
        slab = jnp.clip(slab, 0, patches - 1)
        return lax.dynamic_slice_in_dim(parts, place(slab) * rows, rows, 0) * LIFT

    up = down = None
    steps = []
    for step in range(1, patches):
        send_up = mine(patches - step + me)
        send_down = mine(step - patches + me)
        if step > 1:
            send_up = send_up + up.astype(F32)
            send_down = send_down + down.astype(F32)
        send_up, send_down = send_up.astype(F16), send_down.astype(F16)
        if step == 1 and after is not None:
            send_up, send_down, _ = lax.optimization_barrier((send_up, send_down, after))
        up = lax.ppermute(send_up, "patch", [(i, i + 1) for i in range(step)])
        down = lax.ppermute(send_down, "patch", [(patches - 1 - i, patches - 2 - i) for i in range(step)])
        steps.append((up, down))
    total = mine(me)
    if patches > 1:
        total = total + (up.astype(F32) + down.astype(F32))
    return (total * (1.0 / LIFT)).astype(BF16), steps


def attend_head(patches, rows, scale, me_ref, query_ref, stale_ref, fresh_ref, out_ref):
    me = me_ref[0]
    query = query_ref[...]
    starts = [pl.multiple_of(lax.rem(me + j, patches) * rows, rows) for j in range(1, patches)]
    dims = (((1,), (1,)), ((), ()))
    keys = [fresh_ref[0]] + [stale_ref[0, pl.ds(start, rows), :] for start in starts]
    scores = [lax.dot_general(query, key, dims, preferred_element_type=F32) * scale for key in keys]
    top = functools.reduce(jnp.maximum, [jnp.max(s, axis=-1, keepdims=True) for s in scores])
    total = mixed = None
    values = [fresh_ref[1]] + [stale_ref[1, pl.ds(start, rows), :] for start in starts]
    for s, value in zip(scores, values):
        expo = jnp.exp(s - top)
        count = jnp.sum(expo, axis=-1, keepdims=True)
        part = jnp.dot(expo.astype(BF16), value, preferred_element_type=F32)
        total = count if total is None else total + count
        mixed = part if mixed is None else mixed + part
    out_ref[...] = (mixed / total).astype(BF16)


def attend(query, stale_kv, fresh_kv, patches):
    rows, width = query.shape
    tokens = stale_kv.shape[1]
    me = lax.axis_index("patch").astype(jnp.int32)[None]
    return pl.pallas_call(
        functools.partial(attend_head, patches, rows, 1.0 / HEAD_DIM**0.5),
        out_shape=jax.ShapeDtypeStruct((rows, width), BF16),
        grid_spec=pltpu.PrefetchScalarGridSpec(
            num_scalar_prefetch=1,
            grid=(width // HEAD_DIM,),
            in_specs=[
                pl.BlockSpec((rows, HEAD_DIM), lambda h, me: (0, h)),
                pl.BlockSpec((2, tokens, HEAD_DIM), lambda h, me: (0, 0, h)),
                pl.BlockSpec((2, rows, HEAD_DIM), lambda h, me: (0, 0, h)),
            ],
            out_specs=pl.BlockSpec((rows, HEAD_DIM), lambda h, me: (0, h)),
        ),
        compiler_params=pltpu.CompilerParams(vmem_limit_bytes=32 * 2**20),
        cost_estimate=pl.CostEstimate(
            flops=4 * rows * tokens * width,
            bytes_accessed=4 * (tokens + 2 * rows) * width,
            transcendentals=rows * tokens * (width // HEAD_DIM),
        ),
    )(me, query, stale_kv, fresh_kv)


def product(blocks_ref, heads_ref, w_ref, out_ref):
    out_ref[...] = jnp.dot(heads_ref[...], w_ref[...], preferred_element_type=F32).astype(out_ref.dtype)


def product_plus(blocks_ref, heads_ref, w_ref, got_ref, out_ref):
    total = jnp.dot(heads_ref[...], w_ref[...], preferred_element_type=F32) + got_ref[...].astype(F32)
    out_ref[...] = total.astype(out_ref.dtype)


def project_columns(heads_out, w_out, blocks, count, width, dtype, got=None, got_at=0):
    rows, depth = heads_out.shape
    in_specs = [
        pl.BlockSpec((rows, depth), lambda j, b: (0, 0)),
        pl.BlockSpec((depth, width), lambda j, b: (0, b[j])),
    ]
    operands = [heads_out, w_out]
    if got is not None:
        in_specs.append(pl.BlockSpec((rows, width), lambda j, b: (0, j + got_at)))
        operands.append(got)
    return pl.pallas_call(
        product if got is None else product_plus,
        out_shape=jax.ShapeDtypeStruct((rows, count * width), dtype),
        grid_spec=pltpu.PrefetchScalarGridSpec(
            num_scalar_prefetch=1,
            grid=(count,),
            in_specs=in_specs,
            out_specs=pl.BlockSpec((rows, width), lambda j, b: (0, j)),
        ),
        compiler_params=pltpu.CompilerParams(vmem_limit_bytes=32 * 2**20),
        cost_estimate=pl.CostEstimate(
            flops=2 * rows * depth * count * width,
            bytes_accessed=2 * (depth + rows) * count * width,
            transcendentals=0,
        ),
    )(blocks, *operands)


def sum_columns(heads_out, w_out, ranks):
    rank = lax.axis_index("tensor").astype(jnp.int32)
    core, chip, chips = rank % 2, rank // 2, ranks // 2
    width = w_out.shape[1] // ranks
    order = [(chip + hop) % chips for hop in range(1, chips)] + [chip]
    theirs = jnp.stack([2 * c + 1 - core for c in order])
    ours = jnp.stack([2 * c + core for c in order])
    send = project_columns(heads_out, w_out, theirs, chips, width, BF16)
    got = lax.ppermute(send, "tensor", [(r, r ^ 1) for r in range(ranks)])
    arrived = []
    for hop in range(1, chips):
        block = project_columns(heads_out, w_out, ours[hop - 1 : hop], 1, width, BF16, got, hop - 1)
        pairs = [(r, (r + 2 * hop) % ranks) for r in range(ranks)]
        arrived.append(lax.ppermute(block, "tensor", pairs))
    total = project_columns(heads_out, w_out, ours[chips - 1 :], 1, width, F32, got, chips - 1)
    for block in arrived:
        total = total + block.astype(F32)
    return total.astype(BF16)


def make_shards(patches, ranks):
    def shards(hidden_in, w_query, w_key, w_value, w_out, stale_kv):
        rows = hidden_in.shape[0]
        me = lax.axis_index("patch")
        features, place = spread_features(hidden_in, patches, ranks)

        def project(weight, after=None):
            parts = jnp.dot(features, weight, preferred_element_type=F32)
            return sum_own_slab(parts, rows, place, patches, after)

        key_fresh, key_steps = project(w_key)
        value_fresh, _ = project(w_value)
        query, _ = project(w_query, key_steps[-2] if patches > 2 else None)

        own_stale = lax.dynamic_slice_in_dim(stale_kv, me * rows, rows, 1).astype(F32)
        fresh = jnp.stack([key_fresh, value_fresh]).astype(F32)
        delta = (fresh - own_stale).astype(BF16)
        own_new = (own_stale + delta.astype(F32)).astype(BF16)
        refreshed = lax.all_gather(own_new, "patch", axis=1, tiled=True)
        heads_out = attend(query, stale_kv, own_new, patches)
        return (sum_columns(heads_out, w_out, ranks), refreshed)

    return shards


def solution(mesh):
    in_specs = (
        P(("groups", "patch"), "tensor"),
        P("patch", "tensor"),
        P("patch", "tensor"),
        P("patch", "tensor"),
        P("tensor", None),
        P(None, "groups", "tensor"),
    )
    out_specs = (P(("groups", "patch"), "tensor"), P(None, "groups", "tensor"))
    return jax.shard_map(
        make_shards(mesh.shape["patch"], mesh.shape["tensor"]),
        mesh=mesh,
        in_specs=in_specs,
        out_specs=out_specs,
        check_vma=False,
    )
```

```python
import functools

import jax
import jax.numpy as jnp
from jax import lax
from jax.experimental import pallas as pl
from jax.experimental.pallas import tpu as pltpu
from jax.sharding import PartitionSpec as P

HEAD_DIM = 128
F32 = jnp.float32
BF16 = jnp.bfloat16
F16 = jnp.float16
LIFT = 8.0


def spread_features(hidden):
    features = lax.all_gather(hidden, "tensor", axis=1, tiled=True)
    return lax.all_to_all(features, "patch", split_axis=1, concat_axis=0, tiled=True)


def spread_in_pairs(hidden):
    rank, patch = lax.axis_index("tensor"), lax.axis_index("patch")
    half = hidden.shape[0] // 2
    across = [(r, r ^ 2) for r in range(4)]
    straight = hidden[:half]
    crossing = lax.ppermute(hidden[half:], "tensor", across)
    is_straight = patch // 2 == rank // 2

    def along(block, flip, far):
        pairs = [
            (4 * s + r, 4 * (r ^ flip) + 2 * (r // 2) + s % 2)
            for s in range(4)
            for r in range(4)
            if ((r ^ flip) // 2 != s // 2) == far
        ]
        return lax.ppermute(block, ("patch", "tensor"), pairs)

    def both_slabs(far):
        held = jnp.where(is_straight, along(straight, 0, far), along(crossing, 2, far))
        other = lax.ppermute(held, "tensor", across)
        low = jnp.where(is_straight, held, other)
        high = jnp.where(is_straight, other, held)
        mine = jnp.concatenate([low, high])
        theirs = lax.ppermute(mine, "tensor", [(r, r ^ 1) for r in range(4)])
        return jnp.concatenate([mine, theirs])

    return both_slabs(True), both_slabs(False)


def sum_in_pairs(far, near, weight):
    rank, patch = lax.axis_index("tensor"), lax.axis_index("patch")
    core = rank % 2
    rows, width = far.shape[0] // 2, weight.shape[1]

    def parts(features):
        return (jnp.dot(features, weight, preferred_element_type=F32) * LIFT).reshape(2, rows, width)

    def slab(pair, odd):
        return lax.dynamic_index_in_dim(pair, odd ^ core, 0, keepdims=False)

    far_parts, near_parts = parts(far), parts(near)
    outer = lax.ppermute(far_parts.astype(F16), "patch", [(0, 1), (3, 2)])
    direct = slab(near_parts, 1 - patch % 2).astype(F16)
    direct, outer = lax.optimization_barrier((direct, outer))
    direct = lax.ppermute(direct, "patch", [(0, 1), (1, 0), (2, 3), (3, 2)])
    summed = (far_parts + outer.astype(F32)).astype(F16)
    over = patch // 2
    inner_got = lax.ppermute(slab(summed, over), "patch", [(1, 2), (2, 1)])
    outer_got = lax.ppermute(slab(summed, 1 - over), "patch", [(1, 3), (2, 0)])
    total = slab(near_parts, patch % 2) + direct.astype(F32)
    total = total + jnp.where((patch == 1) | (patch == 2), inner_got, outer_got).astype(F32)
    return (total * (1.0 / LIFT)).astype(BF16)


def sum_own_slab(features, weight, patches):
    me = lax.axis_index("patch")
    rows = features.shape[0] // patches
    parts = jnp.dot(features, weight, preferred_element_type=F32) * LIFT

    def mine(slab):
        slab = jnp.clip(slab, 0, patches - 1)
        return lax.dynamic_slice_in_dim(parts, slab * rows, rows, 0)

    up = down = None
    for step in range(1, patches):
        send_up = mine(patches - step + me)
        send_down = mine(step - patches + me)
        if step > 1:
            send_up = send_up + up.astype(F32)
            send_down = send_down + down.astype(F32)
        up = lax.ppermute(send_up.astype(F16), "patch", [(i, i + 1) for i in range(step)])
        down = lax.ppermute(
            send_down.astype(F16), "patch", [(patches - 1 - i, patches - 2 - i) for i in range(step)]
        )
    total = mine(me)
    if patches > 1:
        total = total + (up.astype(F32) + down.astype(F32))
    return (total * (1.0 / LIFT)).astype(BF16)


def attend_and_project(patches, heads, chips, place_ref, query_ref, stale_ref, key_ref, value_ref, w_ref, send_ref, keep_ref, sums):
    me = place_ref[0]
    rows = query_ref.shape[0]
    width = w_ref.shape[1] // (2 * chips)
    scale = 1.0 / HEAD_DIM**0.5
    starts = [pl.multiple_of(lax.rem(me + j, patches) * rows, rows) for j in range(1, patches)]
    dims = (((1,), (1,)), ((), ()))
    mixed_heads = []
    for h in range(heads):
        columns = slice(h * HEAD_DIM, (h + 1) * HEAD_DIM)
        query = query_ref[:, columns]
        keys = [key_ref[:, columns]] + [stale_ref[0, pl.ds(start, rows), columns] for start in starts]
        values = [value_ref[:, columns]] + [stale_ref[1, pl.ds(start, rows), columns] for start in starts]
        scores = [lax.dot_general(query, key, dims, preferred_element_type=F32) * scale for key in keys]
        top = functools.reduce(jnp.maximum, [jnp.max(s, axis=-1, keepdims=True) for s in scores])
        total = mixed = None
        for s, value in zip(scores, values):
            expo = jnp.exp(s - top)
            count = jnp.sum(expo, axis=-1, keepdims=True)
            part = jnp.dot(expo.astype(BF16), value, preferred_element_type=F32)
            total = count if total is None else total + count
            mixed = part if mixed is None else mixed + part
        mixed_heads.append((mixed / total).astype(BF16))
    heads_out = jnp.concatenate(mixed_heads, axis=1) if heads > 1 else mixed_heads[0]
    product = jnp.dot(heads_out, w_ref[...], preferred_element_type=F32)

    @pl.when(pl.program_id(0) == 0)
    def _():
        sums[...] = product

    @pl.when(pl.program_id(0) > 0)
    def _():
        sums[...] += product

    @pl.when(pl.program_id(0) == pl.num_programs(0) - 1)
    def _():
        for j in range(chips):
            theirs = pl.multiple_of(place_ref[1 + j] * width, width)
            ours = pl.multiple_of(place_ref[1 + chips + j] * width, width)
            send_ref[:, j * width : (j + 1) * width] = sums[:, pl.ds(theirs, width)].astype(BF16)
            keep_ref[:, j * width : (j + 1) * width] = sums[:, pl.ds(ours, width)]


def attend(query, stale_kv, key_new, value_new, w_out, patches, ranks):
    rows, depth = query.shape
    tokens, model = stale_kv.shape[1], w_out.shape[1]
    rank = lax.axis_index("tensor").astype(jnp.int32)
    core, chip, chips = rank % 2, rank // 2, ranks // 2
    width = model // ranks
    order = [(chip + hop) % chips for hop in range(1, chips)] + [chip]
    me = lax.axis_index("patch").astype(jnp.int32)
    place = jnp.stack([me] + [2 * c + 1 - core for c in order] + [2 * c + core for c in order])
    heads = 2 if depth % (2 * HEAD_DIM) == 0 else 1
    block = heads * HEAD_DIM
    send, keep = pl.pallas_call(
        functools.partial(attend_and_project, patches, heads, chips),
        out_shape=(
            jax.ShapeDtypeStruct((rows, chips * width), BF16),
            jax.ShapeDtypeStruct((rows, chips * width), F32),
        ),
        grid_spec=pltpu.PrefetchScalarGridSpec(
            num_scalar_prefetch=1,
            grid=(depth // block,),
            in_specs=[
                pl.BlockSpec((rows, block), lambda h, p: (0, h)),
                pl.BlockSpec((2, tokens, block), lambda h, p: (0, 0, h)),
                pl.BlockSpec((rows, block), lambda h, p: (0, h)),
                pl.BlockSpec((rows, block), lambda h, p: (0, h)),
                pl.BlockSpec((block, model), lambda h, p: (h, 0)),
            ],
            out_specs=(
                pl.BlockSpec((rows, chips * width), lambda h, p: (0, 0)),
                pl.BlockSpec((rows, chips * width), lambda h, p: (0, 0)),
            ),
            scratch_shapes=[pltpu.VMEM((rows, model), F32)],
        ),
        compiler_params=pltpu.CompilerParams(vmem_limit_bytes=48 * 2**20),
        cost_estimate=pl.CostEstimate(
            flops=4 * rows * tokens * depth + 2 * rows * depth * model,
            bytes_accessed=4 * tokens * depth + 2 * depth * model + 6 * rows * chips * width,
            transcendentals=rows * tokens * (depth // HEAD_DIM),
        ),
    )(place, query, stale_kv, key_new, value_new, w_out)
    got = lax.ppermute(send, "tensor", [(r, r ^ 1) for r in range(ranks)])

    def summed(j):
        return keep[:, j * width : (j + 1) * width] + got[:, j * width : (j + 1) * width].astype(F32)

    arrived = []
    for hop in range(1, chips):
        pairs = [(r, (r + 2 * hop) % ranks) for r in range(ranks)]
        arrived.append(lax.ppermute(summed(hop - 1).astype(BF16), "tensor", pairs))
    total = summed(chips - 1)
    for block in arrived:
        total = total + block.astype(F32)
    return total.astype(BF16)


def make_shards(patches, ranks):
    def shards(hidden_in, w_query, w_key, w_value, w_out, stale_kv):
        rows = hidden_in.shape[0]
        me = lax.axis_index("patch")
        if patches == ranks == 4:
            far, near = spread_in_pairs(hidden_in)
            project = functools.partial(sum_in_pairs, far, near)
        else:
            features = spread_features(hidden_in)
            project = lambda weight: sum_own_slab(features, weight, patches)
        own_stale = lax.dynamic_slice_in_dim(stale_kv, me * rows, rows, 1).astype(F32)

        def refresh(fresh, stale):
            fresh = lax.reduce_precision(fresh.astype(F32), 8, 7)
            delta = lax.reduce_precision(fresh - stale, 8, 7)
            return (stale + delta).astype(BF16)

        key_new = refresh(project(w_key), own_stale[0])
        keys_all = lax.all_gather(key_new, "patch", axis=0, tiled=True)
        query = project(w_query)
        value_new = refresh(project(w_value), own_stale[1])
        values_all = lax.all_gather(value_new, "patch", axis=0, tiled=True)
        refreshed = jnp.broadcast_to(keys_all[None], stale_kv.shape).at[1].set(values_all)
        attended = attend(query, stale_kv, key_new, value_new, w_out, patches, ranks)
        return (attended, refreshed)

    return shards


def solution(mesh):
    in_specs = (
        P(("groups", "patch"), "tensor"),
        P("patch", "tensor"),
        P("patch", "tensor"),
        P("patch", "tensor"),
        P("tensor", None),
        P(None, "groups", "tensor"),
    )
    out_specs = (P(("groups", "patch"), "tensor"), P(None, "groups", "tensor"))
    return jax.shard_map(
        make_shards(mesh.shape["patch"], mesh.shape["tensor"]),
        mesh=mesh,
        in_specs=in_specs,
        out_specs=out_specs,
        check_vma=False,
    )
```

```python
import functools

import jax
import jax.numpy as jnp
from jax import lax
from jax.experimental import pallas as pl
from jax.experimental.pallas import tpu as pltpu
from jax.sharding import PartitionSpec as P

HEAD_DIM = 128
F32 = jnp.float32
BF16 = jnp.bfloat16
F16 = jnp.float16
LIFT = 8.0


def spread_features(hidden):
    features = lax.all_gather(hidden, "tensor", axis=1, tiled=True)
    return lax.all_to_all(features, "patch", split_axis=1, concat_axis=0, tiled=True)


def spread_in_pairs(hidden):
    rank, patch = lax.axis_index("tensor"), lax.axis_index("patch")
    half = hidden.shape[0] // 2
    across = [(r, r ^ 2) for r in range(4)]
    straight = hidden[:half]
    crossing = lax.ppermute(hidden[half:], "tensor", across)
    is_straight = patch // 2 == rank // 2

    def along(block, flip, far):
        pairs = [
            (4 * s + r, 4 * (r ^ flip) + 2 * (r // 2) + s % 2)
            for s in range(4)
            for r in range(4)
            if ((r ^ flip) // 2 != s // 2) == far
        ]
        return lax.ppermute(block, ("patch", "tensor"), pairs)

    def both_slabs(far):
        held = jnp.where(is_straight, along(straight, 0, far), along(crossing, 2, far))
        other = lax.ppermute(held, "tensor", across)
        low = jnp.where(is_straight, held, other)
        high = jnp.where(is_straight, other, held)
        mine = jnp.concatenate([low, high])
        theirs = lax.ppermute(mine, "tensor", [(r, r ^ 1) for r in range(4)])
        return jnp.concatenate([mine, theirs])

    return both_slabs(True), both_slabs(False)


def after(value, *earlier):
    return lax.optimization_barrier((value, *earlier))[0]


class PairSum:
    def __init__(self, far, near, weight):
        self.patch = lax.axis_index("patch")
        self.core = lax.axis_index("tensor") % 2
        self.far, self.near = self.parts(far, weight), self.parts(near, weight)

    def parts(self, features, weight):
        product = jnp.dot(features, weight, preferred_element_type=F32) * LIFT
        return product.reshape(2, features.shape[0] // 2, weight.shape[1])

    def slab(self, pair, odd):
        return lax.dynamic_index_in_dim(pair, odd ^ self.core, 0, keepdims=False)

    def to_inner(self, *earlier):
        send = after(self.far.astype(F16), *earlier)
        self.outer = lax.ppermute(send, "patch", [(0, 1), (3, 2)])

    def send_on(self):
        direct = after(self.slab(self.near, 1 - self.patch % 2).astype(F16), self.outer)
        summed = (self.far + self.outer.astype(F32)).astype(F16)
        over = self.patch // 2
        self.inner_got = lax.ppermute(self.slab(summed, over), "patch", [(1, 2), (2, 1)])
        self.outer_got = lax.ppermute(self.slab(summed, 1 - over), "patch", [(1, 3), (2, 0)])
        self.direct = lax.ppermute(direct, "patch", [(0, 1), (1, 0), (2, 3), (3, 2)])

    def total(self, *earlier):
        direct = after(self.direct, *earlier)
        is_inner = (self.patch == 1) | (self.patch == 2)
        total = self.slab(self.near, self.patch % 2) + direct.astype(F32)
        total = total + jnp.where(is_inner, self.inner_got, self.outer_got).astype(F32)
        return (total * (1.0 / LIFT)).astype(BF16)


class PairGather:
    def __init__(self, own):
        self.own = own
        self.mate = lax.ppermute(own, "patch", [(0, 1), (1, 0), (2, 3), (3, 2)])
        self.across = lax.ppermute(own, "patch", [(1, 2), (2, 1)])

    def into(self, whole, index, earlier):
        patch = lax.axis_index("patch")
        rows = self.own.shape[0]
        is_inner = (patch == 1) | (patch == 2)
        outward = [(1, 0), (2, 3)]
        across_mate = lax.ppermute(self.mate, "patch", [(1, 2), (2, 1)])
        far_inner = jnp.where(is_inner, self.across, lax.ppermute(self.across, "patch", outward))
        last = lax.ppermute(after(across_mate, earlier), "patch", outward)
        far_outer = jnp.where(is_inner, across_mate, last)
        own = after(self.own, self.mate)
        low = patch < 2
        slabs = (patch, patch ^ 1, jnp.where(low, 2, 1), jnp.where(low, 3, 0))
        for slab, block in zip(slabs, (own, self.mate, far_inner, far_outer)):
            whole = lax.dynamic_update_slice(whole, block[None], (index, slab * rows, 0))
        return whole


def sum_own_slab(features, weight, patches):
    me = lax.axis_index("patch")
    rows = features.shape[0] // patches
    parts = jnp.dot(features, weight, preferred_element_type=F32) * LIFT

    def mine(slab):
        slab = jnp.clip(slab, 0, patches - 1)
        return lax.dynamic_slice_in_dim(parts, slab * rows, rows, 0)

    up = down = None
    for step in range(1, patches):
        send_up = mine(patches - step + me)
        send_down = mine(step - patches + me)
        if step > 1:
            send_up = send_up + up.astype(F32)
            send_down = send_down + down.astype(F32)
        up = lax.ppermute(send_up.astype(F16), "patch", [(i, i + 1) for i in range(step)])
        down = lax.ppermute(
            send_down.astype(F16), "patch", [(patches - 1 - i, patches - 2 - i) for i in range(step)]
        )
    total = mine(me)
    if patches > 1:
        total = total + (up.astype(F32) + down.astype(F32))
    return (total * (1.0 / LIFT)).astype(BF16)


def attend_and_project(patches, heads, chips, place_ref, query_ref, stale_ref, key_ref, value_ref, w_ref, send_ref, keep_ref, sums):
    me = place_ref[0]
    rows = query_ref.shape[0]
    width = w_ref.shape[1] // (2 * chips)
    scale = 1.0 / HEAD_DIM**0.5
    starts = [pl.multiple_of(lax.rem(me + j, patches) * rows, rows) for j in range(1, patches)]
    dims = (((1,), (1,)), ((), ()))
    mixed_heads = []
    for h in range(heads):
        columns = slice(h * HEAD_DIM, (h + 1) * HEAD_DIM)
        query = query_ref[:, columns]
        keys = [key_ref[:, columns]] + [stale_ref[0, pl.ds(start, rows), columns] for start in starts]
        values = [value_ref[:, columns]] + [stale_ref[1, pl.ds(start, rows), columns] for start in starts]
        scores = [lax.dot_general(query, key, dims, preferred_element_type=F32) * scale for key in keys]
        top = functools.reduce(jnp.maximum, [jnp.max(s, axis=-1, keepdims=True) for s in scores])
        total = mixed = None
        for s, value in zip(scores, values):
            expo = jnp.exp(s - top)
            count = jnp.sum(expo, axis=-1, keepdims=True)
            part = jnp.dot(expo.astype(BF16), value, preferred_element_type=F32)
            total = count if total is None else total + count
            mixed = part if mixed is None else mixed + part
        mixed_heads.append((mixed / total).astype(BF16))
    heads_out = jnp.concatenate(mixed_heads, axis=1) if heads > 1 else mixed_heads[0]
    product = jnp.dot(heads_out, w_ref[...], preferred_element_type=F32)

    @pl.when(pl.program_id(0) == 0)
    def _():
        sums[...] = product

    @pl.when(pl.program_id(0) > 0)
    def _():
        sums[...] += product

    @pl.when(pl.program_id(0) == pl.num_programs(0) - 1)
    def _():
        for j in range(chips):
            theirs = pl.multiple_of(place_ref[1 + j] * width, width)
            ours = pl.multiple_of(place_ref[1 + chips + j] * width, width)
            send_ref[:, j * width : (j + 1) * width] = sums[:, pl.ds(theirs, width)].astype(BF16)
            keep_ref[:, j * width : (j + 1) * width] = sums[:, pl.ds(ours, width)]


def attend(query, stale_kv, key_new, value_new, w_out, patches, ranks):
    rows, depth = query.shape
    tokens, model = stale_kv.shape[1], w_out.shape[1]
    rank = lax.axis_index("tensor").astype(jnp.int32)
    core, chip, chips = rank % 2, rank // 2, ranks // 2
    width = model // ranks
    order = [(chip + hop) % chips for hop in range(1, chips)] + [chip]
    me = lax.axis_index("patch").astype(jnp.int32)
    place = jnp.stack([me] + [2 * c + 1 - core for c in order] + [2 * c + core for c in order])
    heads = 2 if depth % (2 * HEAD_DIM) == 0 else 1
    block = heads * HEAD_DIM
    send, keep = pl.pallas_call(
        functools.partial(attend_and_project, patches, heads, chips),
        out_shape=(
            jax.ShapeDtypeStruct((rows, chips * width), BF16),
            jax.ShapeDtypeStruct((rows, chips * width), F32),
        ),
        grid_spec=pltpu.PrefetchScalarGridSpec(
            num_scalar_prefetch=1,
            grid=(depth // block,),
            in_specs=[
                pl.BlockSpec((rows, block), lambda h, p: (0, h)),
                pl.BlockSpec((2, tokens, block), lambda h, p: (0, 0, h)),
                pl.BlockSpec((rows, block), lambda h, p: (0, h)),
                pl.BlockSpec((rows, block), lambda h, p: (0, h)),
                pl.BlockSpec((block, model), lambda h, p: (h, 0)),
            ],
            out_specs=(
                pl.BlockSpec((rows, chips * width), lambda h, p: (0, 0)),
                pl.BlockSpec((rows, chips * width), lambda h, p: (0, 0)),
            ),
            scratch_shapes=[pltpu.VMEM((rows, model), F32)],
        ),
        compiler_params=pltpu.CompilerParams(vmem_limit_bytes=48 * 2**20),
        cost_estimate=pl.CostEstimate(
            flops=4 * rows * tokens * depth + 2 * rows * depth * model,
            bytes_accessed=4 * tokens * depth + 2 * depth * model + 6 * rows * chips * width,
            transcendentals=rows * tokens * (depth // HEAD_DIM),
        ),
    )(place, query, stale_kv, key_new, value_new, w_out)
    got = lax.ppermute(send, "tensor", [(r, r ^ 1) for r in range(ranks)])

    def summed(j):
        return keep[:, j * width : (j + 1) * width] + got[:, j * width : (j + 1) * width].astype(F32)

    arrived = []
    for hop in range(1, chips):
        pairs = [(r, (r + 2 * hop) % ranks) for r in range(ranks)]
        arrived.append(lax.ppermute(summed(hop - 1).astype(BF16), "tensor", pairs))
    total = summed(chips - 1)
    for block in arrived:
        total = total + block.astype(F32)
    return total.astype(BF16), got


def make_shards(patches, ranks):
    def shards(hidden_in, w_query, w_key, w_value, w_out, stale_kv):
        rows = hidden_in.shape[0]
        me = lax.axis_index("patch")
        own_stale = lax.dynamic_slice_in_dim(stale_kv, me * rows, rows, 1).astype(F32)

        def refresh(fresh, stale):
            fresh = lax.reduce_precision(fresh.astype(F32), 8, 7)
            delta = lax.reduce_precision(fresh - stale, 8, 7)
            return (stale + delta).astype(BF16)

        def gather(own):
            return lax.all_gather(own, "patch", axis=0, tiled=True)

        if patches == ranks == 4:
            far, near = spread_in_pairs(hidden_in)
            sums = [PairSum(far, near, weight) for weight in (w_key, w_value, w_query)]
            keys, values, queries = sums
            keys.to_inner()
            values.to_inner()
            queries.to_inner(keys.outer)
            for each in sums:
                each.send_on()
            key_new = refresh(keys.total(), own_stale[0])
            keys_all = gather(key_new)
            value_new = refresh(values.total(key_new, queries.outer), own_stale[1])
            gathered = PairGather(value_new)
            query = after(queries.total(keys_all), gathered.mate, gathered.across)
        else:
            features = spread_features(hidden_in)
            key_new, value_new = (
                refresh(sum_own_slab(features, weight, patches), own_stale[i])
                for i, weight in enumerate((w_key, w_value))
            )
            query = sum_own_slab(features, w_query, patches)
        attended, got = attend(query, stale_kv, key_new, value_new, w_out, patches, ranks)
        if patches == ranks == 4:
            refreshed = gathered.into(jnp.broadcast_to(keys_all[None], stale_kv.shape), 1, got)
        else:
            refreshed = jnp.stack([gather(key_new), gather(value_new)])
        return (attended, refreshed)

    return shards


def solution(mesh):
    in_specs = (
        P(("groups", "patch"), "tensor"),
        P("patch", "tensor"),
        P("patch", "tensor"),
        P("patch", "tensor"),
        P("tensor", None),
        P(None, "groups", "tensor"),
    )
    out_specs = (P(("groups", "patch"), "tensor"), P(None, "groups", "tensor"))
    return jax.shard_map(
        make_shards(mesh.shape["patch"], mesh.shape["tensor"]),
        mesh=mesh,
        in_specs=in_specs,
        out_specs=out_specs,
        check_vma=False,
    )
```

```python
import functools

import jax
import jax.numpy as jnp
from jax import lax
from jax.experimental import pallas as pl
from jax.experimental.pallas import tpu as pltpu
from jax.sharding import PartitionSpec as P

HEAD_DIM = 128
F32 = jnp.float32
BF16 = jnp.bfloat16
F16 = jnp.float16
LIFT = 8.0


def spread_features(hidden):
    features = lax.all_gather(hidden, "tensor", axis=1, tiled=True)
    return lax.all_to_all(features, "patch", split_axis=1, concat_axis=0, tiled=True)


def spread_in_pairs(hidden):
    rank, patch = lax.axis_index("tensor"), lax.axis_index("patch")
    half = hidden.shape[0] // 2
    across = [(r, r ^ 2) for r in range(4)]
    straight = hidden[:half]
    crossing = lax.ppermute(hidden[half:], "tensor", across)
    is_straight = patch // 2 == rank // 2

    def along(block, flip, far):
        pairs = [
            (4 * s + r, 4 * (r ^ flip) + 2 * (r // 2) + s % 2)
            for s in range(4)
            for r in range(4)
            if ((r ^ flip) // 2 != s // 2) == far
        ]
        return lax.ppermute(block, ("patch", "tensor"), pairs)

    def both_slabs(far):
        held = jnp.where(is_straight, along(straight, 0, far), along(crossing, 2, far))
        other = lax.ppermute(held, "tensor", across)
        low = jnp.where(is_straight, held, other)
        high = jnp.where(is_straight, other, held)
        mine = jnp.concatenate([low, high])
        theirs = lax.ppermute(mine, "tensor", [(r, r ^ 1) for r in range(4)])
        return jnp.concatenate([mine, theirs])

    return both_slabs(True), both_slabs(False)


def after(value, *earlier):
    if not earlier:
        return value
    return lax.optimization_barrier((value, *earlier))[0]


class PairSum:
    def __init__(self, far, near, weight):
        self.patch = lax.axis_index("patch")
        self.core = lax.axis_index("tensor") % 2
        self.far, self.near = self.parts(far, weight), self.parts(near, weight)

    def parts(self, features, weight):
        product = (jnp.dot(features, weight, preferred_element_type=F32) * LIFT).astype(F16)
        return product.reshape(2, features.shape[0] // 2, weight.shape[1])

    def slab(self, pair, odd):
        return lax.dynamic_index_in_dim(pair, odd ^ self.core, 0, keepdims=False)

    def to_inner(self, *earlier):
        self.outer = lax.ppermute(after(self.far, *earlier), "patch", [(0, 1), (3, 2)])

    def send_on(self, *earlier):
        outer, *earlier = lax.optimization_barrier((self.outer, *earlier))
        direct = after(self.slab(self.near, 1 - self.patch % 2), outer)
        summed = (self.far.astype(F32) + outer.astype(F32)).astype(F16)
        over = self.patch // 2
        self.inner_got = lax.ppermute(self.slab(summed, over), "patch", [(1, 2), (2, 1)])
        self.outer_got = lax.ppermute(self.slab(summed, 1 - over), "patch", [(1, 3), (2, 0)])
        self.direct = lax.ppermute(direct, "patch", [(0, 1), (1, 0), (2, 3), (3, 2)])

    def total(self, *earlier):
        direct = after(self.direct, *earlier)
        is_inner = (self.patch == 1) | (self.patch == 2)
        total = self.slab(self.near, self.patch % 2).astype(F32) + direct.astype(F32)
        total = total + jnp.where(is_inner, self.inner_got, self.outer_got).astype(F32)
        return (total * (1.0 / LIFT)).astype(BF16)


class PairGather:
    def __init__(self, own):
        self.own = own
        self.mate = lax.ppermute(own, "patch", [(0, 1), (1, 0), (2, 3), (3, 2)])
        self.across = lax.ppermute(own, "patch", [(1, 2), (2, 1)])

    def into(self, whole, index, earlier):
        patch = lax.axis_index("patch")
        rows = self.own.shape[0]
        is_inner = (patch == 1) | (patch == 2)
        outward = [(1, 0), (2, 3)]
        across_mate = lax.ppermute(self.mate, "patch", [(1, 2), (2, 1)])
        far_inner = jnp.where(is_inner, self.across, lax.ppermute(self.across, "patch", outward))
        last = lax.ppermute(after(across_mate, earlier), "patch", outward)
        far_outer = jnp.where(is_inner, across_mate, last)
        own = after(self.own, self.mate)
        low = patch < 2
        slabs = (patch, patch ^ 1, jnp.where(low, 2, 1), jnp.where(low, 3, 0))
        for slab, block in zip(slabs, (own, self.mate, far_inner, far_outer)):
            whole = lax.dynamic_update_slice(whole, block[None], (index, slab * rows, 0))
        return whole


def sum_own_slab(features, weight, patches):
    me = lax.axis_index("patch")
    rows = features.shape[0] // patches
    parts = jnp.dot(features, weight, preferred_element_type=F32) * LIFT

    def mine(slab):
        slab = jnp.clip(slab, 0, patches - 1)
        return lax.dynamic_slice_in_dim(parts, slab * rows, rows, 0)

    up = down = None
    for step in range(1, patches):
        send_up = mine(patches - step + me)
        send_down = mine(step - patches + me)
        if step > 1:
            send_up = send_up + up.astype(F32)
            send_down = send_down + down.astype(F32)
        up = lax.ppermute(send_up.astype(F16), "patch", [(i, i + 1) for i in range(step)])
        down = lax.ppermute(
            send_down.astype(F16), "patch", [(patches - 1 - i, patches - 2 - i) for i in range(step)]
        )
    total = mine(me)
    if patches > 1:
        total = total + (up.astype(F32) + down.astype(F32))
    return (total * (1.0 / LIFT)).astype(BF16)


def attend_and_project(patches, heads, chips, place_ref, query_ref, stale_ref, key_ref, value_ref, w_ref, send_ref, keep_ref, sums):
    me = place_ref[0]
    rows = query_ref.shape[0]
    width = w_ref.shape[1] // (2 * chips)
    scale = 1.0 / HEAD_DIM**0.5
    starts = [pl.multiple_of(lax.rem(me + j, patches) * rows, rows) for j in range(1, patches)]
    dims = (((1,), (1,)), ((), ()))
    mixed_heads = []
    for h in range(heads):
        columns = slice(h * HEAD_DIM, (h + 1) * HEAD_DIM)
        query = query_ref[:, columns]
        keys = [key_ref[:, columns]] + [stale_ref[0, pl.ds(start, rows), columns] for start in starts]
        values = [value_ref[:, columns]] + [stale_ref[1, pl.ds(start, rows), columns] for start in starts]
        scores = [lax.dot_general(query, key, dims, preferred_element_type=F32) * scale for key in keys]
        top = functools.reduce(jnp.maximum, [jnp.max(s, axis=-1, keepdims=True) for s in scores])
        total = mixed = None
        for s, value in zip(scores, values):
            expo = jnp.exp(s - top)
            count = jnp.sum(expo, axis=-1, keepdims=True)
            part = jnp.dot(expo.astype(BF16), value, preferred_element_type=F32)
            total = count if total is None else total + count
            mixed = part if mixed is None else mixed + part
        mixed_heads.append((mixed / total).astype(BF16))
    heads_out = jnp.concatenate(mixed_heads, axis=1) if heads > 1 else mixed_heads[0]
    product = jnp.dot(heads_out, w_ref[...], preferred_element_type=F32)

    @pl.when(pl.program_id(0) == 0)
    def _():
        sums[...] = product

    @pl.when(pl.program_id(0) > 0)
    def _():
        sums[...] += product

    @pl.when(pl.program_id(0) == pl.num_programs(0) - 1)
    def _():
        for j in range(chips):
            theirs = pl.multiple_of(place_ref[1 + j] * width, width)
            ours = pl.multiple_of(place_ref[1 + chips + j] * width, width)
            send_ref[:, j * width : (j + 1) * width] = sums[:, pl.ds(theirs, width)].astype(BF16)
            keep_ref[:, j * width : (j + 1) * width] = sums[:, pl.ds(ours, width)]


def attend(query, stale_kv, key_new, value_new, w_out, patches, ranks):
    rows, depth = query.shape
    tokens, model = stale_kv.shape[1], w_out.shape[1]
    rank = lax.axis_index("tensor").astype(jnp.int32)
    core, chip, chips = rank % 2, rank // 2, ranks // 2
    width = model // ranks
    order = [(chip + hop) % chips for hop in range(1, chips)] + [chip]
    me = lax.axis_index("patch").astype(jnp.int32)
    place = jnp.stack([me] + [2 * c + 1 - core for c in order] + [2 * c + core for c in order])
    heads = 2 if depth % (2 * HEAD_DIM) == 0 else 1
    block = heads * HEAD_DIM
    send, keep = pl.pallas_call(
        functools.partial(attend_and_project, patches, heads, chips),
        out_shape=(
            jax.ShapeDtypeStruct((rows, chips * width), BF16),
            jax.ShapeDtypeStruct((rows, chips * width), F32),
        ),
        grid_spec=pltpu.PrefetchScalarGridSpec(
            num_scalar_prefetch=1,
            grid=(depth // block,),
            in_specs=[
                pl.BlockSpec((rows, block), lambda h, p: (0, h)),
                pl.BlockSpec((2, tokens, block), lambda h, p: (0, 0, h)),
                pl.BlockSpec((rows, block), lambda h, p: (0, h)),
                pl.BlockSpec((rows, block), lambda h, p: (0, h)),
                pl.BlockSpec((block, model), lambda h, p: (h, 0)),
            ],
            out_specs=(
                pl.BlockSpec((rows, chips * width), lambda h, p: (0, 0)),
                pl.BlockSpec((rows, chips * width), lambda h, p: (0, 0)),
            ),
            scratch_shapes=[pltpu.VMEM((rows, model), F32)],
        ),
        compiler_params=pltpu.CompilerParams(vmem_limit_bytes=48 * 2**20),
        cost_estimate=pl.CostEstimate(
            flops=4 * rows * tokens * depth + 2 * rows * depth * model,
            bytes_accessed=4 * tokens * depth + 2 * depth * model + 6 * rows * chips * width,
            transcendentals=rows * tokens * (depth // HEAD_DIM),
        ),
    )(place, query, stale_kv, key_new, value_new, w_out)
    got = lax.ppermute(send, "tensor", [(r, r ^ 1) for r in range(ranks)])

    def summed(j):
        return keep[:, j * width : (j + 1) * width] + got[:, j * width : (j + 1) * width].astype(F32)

    arrived = []
    for hop in range(1, chips):
        pairs = [(r, (r + 2 * hop) % ranks) for r in range(ranks)]
        arrived.append(lax.ppermute(summed(hop - 1).astype(BF16), "tensor", pairs))
    total = summed(chips - 1)
    for block in arrived:
        total = total + block.astype(F32)
    return total.astype(BF16), got


def make_shards(patches, ranks):
    def shards(hidden_in, w_query, w_key, w_value, w_out, stale_kv):
        rows = hidden_in.shape[0]
        me = lax.axis_index("patch")
        own_stale = lax.dynamic_slice_in_dim(stale_kv, me * rows, rows, 1).astype(F32)

        def refresh(fresh, stale):
            fresh = lax.reduce_precision(fresh.astype(F32), 8, 7)
            delta = lax.reduce_precision(fresh - stale, 8, 7)
            return (stale + delta).astype(BF16)

        def gather(own):
            return lax.all_gather(own, "patch", axis=0, tiled=True)

        if patches == ranks == 4:
            far, near = spread_in_pairs(hidden_in)
            sums = [PairSum(far, near, weight) for weight in (w_key, w_value, w_query)]
            keys, values, queries = sums
            keys.to_inner()
            values.to_inner()
            queries.to_inner(keys.outer)
            keys.send_on(values.outer)
            values.send_on(queries.outer)
            queries.send_on()
            key_new = refresh(keys.total(), own_stale[0])
            keys_all = gather(key_new)
            value_new = refresh(values.total(key_new), own_stale[1])
            gathered = PairGather(value_new)
            query = after(queries.total(keys_all), gathered.mate, gathered.across)
        else:
            features = spread_features(hidden_in)
            key_new, value_new = (
                refresh(sum_own_slab(features, weight, patches), own_stale[i])
                for i, weight in enumerate((w_key, w_value))
            )
            query = sum_own_slab(features, w_query, patches)
        attended, got = attend(query, stale_kv, key_new, value_new, w_out, patches, ranks)
        if patches == ranks == 4:
            refreshed = gathered.into(jnp.broadcast_to(keys_all[None], stale_kv.shape), 1, got)
        else:
            refreshed = jnp.stack([gather(key_new), gather(value_new)])
        return (attended, refreshed)

    return shards


def solution(mesh):
    in_specs = (
        P(("groups", "patch"), "tensor"),
        P("patch", "tensor"),
        P("patch", "tensor"),
        P("patch", "tensor"),
        P("tensor", None),
        P(None, "groups", "tensor"),
    )
    out_specs = (P(("groups", "patch"), "tensor"), P(None, "groups", "tensor"))
    return jax.shard_map(
        make_shards(mesh.shape["patch"], mesh.shape["tensor"]),
        mesh=mesh,
        in_specs=in_specs,
        out_specs=out_specs,
        check_vma=False,
    )
```

```python
import functools

import jax
import jax.numpy as jnp
from jax import lax
from jax.experimental import pallas as pl
from jax.experimental.pallas import tpu as pltpu
from jax.sharding import PartitionSpec as P

HEAD_DIM = 128
F32 = jnp.float32
BF16 = jnp.bfloat16
F16 = jnp.float16
LIFT = 8.0


def spread_features(hidden):
    features = lax.all_gather(hidden, "tensor", axis=1, tiled=True)
    return lax.all_to_all(features, "patch", split_axis=1, concat_axis=0, tiled=True)


def spread_in_pairs(hidden):
    rank, patch = lax.axis_index("tensor"), lax.axis_index("patch")
    half = hidden.shape[0] // 2
    across = [(r, r ^ 2) for r in range(4)]
    straight = hidden[:half]
    crossing = lax.ppermute(hidden[half:], "tensor", across)
    is_straight = patch // 2 == rank // 2

    def along(block, flip, far):
        pairs = [
            (4 * s + r, 4 * (r ^ flip) + 2 * (r // 2) + s % 2)
            for s in range(4)
            for r in range(4)
            if ((r ^ flip) // 2 != s // 2) == far
        ]
        return lax.ppermute(block, ("patch", "tensor"), pairs)

    def both_slabs(far):
        held = jnp.where(is_straight, along(straight, 0, far), along(crossing, 2, far))
        other = lax.ppermute(held, "tensor", across)
        low = jnp.where(is_straight, held, other)
        high = jnp.where(is_straight, other, held)
        mine = jnp.concatenate([low, high])
        theirs = lax.ppermute(mine, "tensor", [(r, r ^ 1) for r in range(4)])
        return jnp.concatenate([mine, theirs])

    return both_slabs(True), both_slabs(False)


def sum_in_pairs(far, near, weight):
    patch, core = lax.axis_index("patch"), lax.axis_index("tensor") % 2

    def project(features):
        product = (jnp.dot(features, weight, preferred_element_type=F32) * LIFT).astype(F16)
        return product.reshape(2, features.shape[0] // 2, weight.shape[1])

    far, near = project(far), project(near)

    def mine(slab, step):
        slab = jnp.clip(slab, 0, 3)
        place = (slab % 2) ^ core
        part = lax.dynamic_index_in_dim(far, place, 0, keepdims=False)
        if step == 3:
            other = lax.dynamic_index_in_dim(near, place, 0, keepdims=False)
            part = jnp.where(slab // 2 == patch // 2, other, part)
        return part

    up = down = None
    for step in range(1, 4):
        send_up, send_down = mine(4 - step + patch, step), mine(step - 4 + patch, step)
        if step > 1:
            send_up = (send_up.astype(F32) + up.astype(F32)).astype(F16)
            send_down = (send_down.astype(F32) + down.astype(F32)).astype(F16)
        up = lax.ppermute(send_up, "patch", [(i, i + 1) for i in range(step)])
        down = lax.ppermute(send_down, "patch", [(3 - i, 2 - i) for i in range(step)])
    own = lax.dynamic_index_in_dim(near, (patch % 2) ^ core, 0, keepdims=False)
    total = own.astype(F32) + (up.astype(F32) + down.astype(F32))
    return (total * (1.0 / LIFT)).astype(BF16)


def sum_own_slab(features, weight, patches):
    me = lax.axis_index("patch")
    rows = features.shape[0] // patches
    parts = jnp.dot(features, weight, preferred_element_type=F32) * LIFT

    def mine(slab):
        slab = jnp.clip(slab, 0, patches - 1)
        return lax.dynamic_slice_in_dim(parts, slab * rows, rows, 0)

    up = down = None
    for step in range(1, patches):
        send_up = mine(patches - step + me)
        send_down = mine(step - patches + me)
        if step > 1:
            send_up = send_up + up.astype(F32)
            send_down = send_down + down.astype(F32)
        up = lax.ppermute(send_up.astype(F16), "patch", [(i, i + 1) for i in range(step)])
        down = lax.ppermute(
            send_down.astype(F16), "patch", [(patches - 1 - i, patches - 2 - i) for i in range(step)]
        )
    total = mine(me)
    if patches > 1:
        total = total + (up.astype(F32) + down.astype(F32))
    return (total * (1.0 / LIFT)).astype(BF16)


def attend_and_project(patches, heads, chips, chunks, place_ref, query_ref, stale_ref, fresh_ref, w_ref, *out_refs):
    *out_refs, sums = out_refs
    send_refs, keep_refs = out_refs[:chunks], out_refs[chunks:]
    me = place_ref[0]
    rows = query_ref.shape[0]
    width = w_ref.shape[1] // (2 * chips)
    scale = 1.0 / HEAD_DIM**0.5
    starts = [pl.multiple_of(lax.rem(me + j, patches) * rows, rows) for j in range(1, patches)]
    dims = (((1,), (1,)), ((), ()))
    mixed_heads = []
    for h in range(heads):
        columns = slice(h * HEAD_DIM, (h + 1) * HEAD_DIM)
        query = query_ref[:, columns]
        keys = [fresh_ref[0, :, columns]] + [stale_ref[0, pl.ds(start, rows), columns] for start in starts]
        values = [fresh_ref[1, :, columns]] + [stale_ref[1, pl.ds(start, rows), columns] for start in starts]
        scores = [lax.dot_general(query, key, dims, preferred_element_type=F32) * scale for key in keys]
        top = functools.reduce(jnp.maximum, [jnp.max(s, axis=-1, keepdims=True) for s in scores])
        total = mixed = None
        for s, value in zip(scores, values):
            expo = jnp.exp(s - top)
            count = jnp.sum(expo, axis=-1, keepdims=True)
            part = jnp.dot(expo.astype(BF16), value, preferred_element_type=F32)
            total = count if total is None else total + count
            mixed = part if mixed is None else mixed + part
        mixed_heads.append((mixed / total).astype(BF16))
    heads_out = jnp.concatenate(mixed_heads, axis=1) if heads > 1 else mixed_heads[0]
    product = jnp.dot(heads_out, w_ref[...], preferred_element_type=F32)

    @pl.when(pl.program_id(0) == 0)
    def _():
        sums[...] = product

    @pl.when(pl.program_id(0) > 0)
    def _():
        sums[...] += product

    @pl.when(pl.program_id(0) == pl.num_programs(0) - 1)
    def _():
        part = width // chunks
        for c in range(chunks):
            for j in range(chips):
                theirs = pl.multiple_of(place_ref[1 + j] * width + c * part, part)
                ours = pl.multiple_of(place_ref[1 + chips + j] * width + c * part, part)
                there = slice(j * part, (j + 1) * part)
                send_refs[c][:, there] = sums[:, pl.ds(theirs, part)].astype(BF16)
                keep_refs[c][:, there] = sums[:, pl.ds(ours, part)]


def attend(query, stale_kv, fresh_kv, w_out, patches, ranks):
    rows, depth = query.shape
    tokens, model = stale_kv.shape[1], w_out.shape[1]
    rank = lax.axis_index("tensor").astype(jnp.int32)
    core, chip, chips = rank % 2, rank // 2, ranks // 2
    width = model // ranks
    order = [(chip + hop) % chips for hop in range(1, chips)] + [chip]
    me = lax.axis_index("patch").astype(jnp.int32)
    place = jnp.stack([me] + [2 * c + 1 - core for c in order] + [2 * c + core for c in order])
    heads = 2 if depth % (2 * HEAD_DIM) == 0 else 1
    block = heads * HEAD_DIM
    chunks = 2 if width % (2 * 128) == 0 else 1
    part = width // chunks
    results = pl.pallas_call(
        functools.partial(attend_and_project, patches, heads, chips, chunks),
        out_shape=[jax.ShapeDtypeStruct((rows, chips * part), BF16)] * chunks
        + [jax.ShapeDtypeStruct((rows, chips * part), F32)] * chunks,
        grid_spec=pltpu.PrefetchScalarGridSpec(
            num_scalar_prefetch=1,
            grid=(depth // block,),
            in_specs=[
                pl.BlockSpec((rows, block), lambda h, p: (0, h)),
                pl.BlockSpec((2, tokens, block), lambda h, p: (0, 0, h)),
                pl.BlockSpec((2, rows, block), lambda h, p: (0, 0, h)),
                pl.BlockSpec((block, model), lambda h, p: (h, 0)),
            ],
            out_specs=[pl.BlockSpec((rows, chips * part), lambda h, p: (0, 0))] * (2 * chunks),
            scratch_shapes=[pltpu.VMEM((rows, model), F32)],
        ),
        compiler_params=pltpu.CompilerParams(vmem_limit_bytes=48 * 2**20),
        cost_estimate=pl.CostEstimate(
            flops=4 * rows * tokens * depth + 2 * rows * depth * model,
            bytes_accessed=4 * tokens * depth + 2 * depth * model + 6 * rows * chips * width,
            transcendentals=rows * tokens * (depth // HEAD_DIM),
        ),
    )(place, query, stale_kv, fresh_kv, w_out)
    across = [(r, r ^ 1) for r in range(ranks)]
    got = [lax.ppermute(send, "tensor", across) for send in results[:chunks]]
    pieces = []
    for mine, theirs in zip(results[chunks:], got):

        def summed(j):
            return mine[:, j * part : (j + 1) * part] + theirs[:, j * part : (j + 1) * part].astype(F32)

        arrived = []
        for hop in range(1, chips):
            pairs = [(r, (r + 2 * hop) % ranks) for r in range(ranks)]
            arrived.append(lax.ppermute(summed(hop - 1).astype(BF16), "tensor", pairs))
        total = summed(chips - 1)
        for piece in arrived:
            total = total + piece.astype(F32)
        pieces.append(total.astype(BF16))
    return jnp.concatenate(pieces, axis=1)


def make_shards(patches, ranks):
    def shards(hidden_in, w_query, w_key, w_value, w_out, stale_kv):
        rows = hidden_in.shape[0]
        me = lax.axis_index("patch")
        own_stale = lax.dynamic_slice_in_dim(stale_kv, me * rows, rows, 1).astype(F32)
        w_both = jnp.concatenate([w_key, w_value], axis=1)
        if patches == ranks == 4:
            far, near = spread_in_pairs(hidden_in)
            both = sum_in_pairs(far, near, w_both)
            query = sum_in_pairs(far, near, w_query)
        else:
            features = spread_features(hidden_in)
            both = sum_own_slab(features, w_both, patches)
            query = sum_own_slab(features, w_query, patches)
        width = w_key.shape[1]
        fresh = lax.reduce_precision(both.astype(F32), 8, 7)
        fresh = jnp.stack([fresh[:, :width], fresh[:, width:]])
        delta = lax.reduce_precision(fresh - own_stale, 8, 7)
        own_new = (own_stale + delta).astype(BF16)
        refreshed = lax.all_gather(own_new, "patch", axis=1, tiled=True)
        attended = attend(query, stale_kv, own_new, w_out, patches, ranks)
        return (attended, refreshed)

    return shards


def solution(mesh):
    in_specs = (
        P(("groups", "patch"), "tensor"),
        P("patch", "tensor"),
        P("patch", "tensor"),
        P("patch", "tensor"),
        P("tensor", None),
        P(None, "groups", "tensor"),
    )
    out_specs = (P(("groups", "patch"), "tensor"), P(None, "groups", "tensor"))
    return jax.shard_map(
        make_shards(mesh.shape["patch"], mesh.shape["tensor"]),
        mesh=mesh,
        in_specs=in_specs,
        out_specs=out_specs,
        check_vma=False,
    )
```

```python
import functools

import jax
import jax.numpy as jnp
from jax import lax
from jax.experimental import pallas as pl
from jax.experimental.pallas import tpu as pltpu
from jax.sharding import PartitionSpec as P

HEAD_DIM = 128
F32 = jnp.float32
BF16 = jnp.bfloat16
F16 = jnp.float16
LIFT = 8.0


def spread_features(hidden):
    features = lax.all_gather(hidden, "tensor", axis=1, tiled=True)
    return lax.all_to_all(features, "patch", split_axis=1, concat_axis=0, tiled=True)


def spread_in_pairs(hidden):
    rank, patch = lax.axis_index("tensor"), lax.axis_index("patch")
    half = hidden.shape[0] // 2
    across = [(r, r ^ 2) for r in range(4)]
    straight = hidden[:half]
    crossing = lax.ppermute(hidden[half:], "tensor", across)
    is_straight = patch // 2 == rank // 2

    def along(block, flip, far):
        pairs = [
            (4 * s + r, 4 * (r ^ flip) + 2 * (r // 2) + s % 2)
            for s in range(4)
            for r in range(4)
            if ((r ^ flip) // 2 != s // 2) == far
        ]
        return lax.ppermute(block, ("patch", "tensor"), pairs)

    def both_slabs(far):
        held = jnp.where(is_straight, along(straight, 0, far), along(crossing, 2, far))
        other = lax.ppermute(held, "tensor", across)
        low = jnp.where(is_straight, held, other)
        high = jnp.where(is_straight, other, held)
        mine = jnp.concatenate([low, high])
        theirs = lax.ppermute(mine, "tensor", [(r, r ^ 1) for r in range(4)])
        return jnp.concatenate([mine, theirs])

    return both_slabs(True), both_slabs(False)


def sum_in_pairs(far, near, weight):
    patch, core = lax.axis_index("patch"), lax.axis_index("tensor") % 2

    def project(features):
        product = (jnp.dot(features, weight, preferred_element_type=F32) * LIFT).astype(F16)
        return product.reshape(2, features.shape[0] // 2, weight.shape[1])

    far, near = project(far), project(near)

    def mine(slab, step):
        slab = jnp.clip(slab, 0, 3)
        place = (slab % 2) ^ core
        part = lax.dynamic_index_in_dim(far, place, 0, keepdims=False)
        if step == 3:
            other = lax.dynamic_index_in_dim(near, place, 0, keepdims=False)
            part = jnp.where(slab // 2 == patch // 2, other, part)
        return part

    up = down = None
    for step in range(1, 4):
        send_up, send_down = mine(4 - step + patch, step), mine(step - 4 + patch, step)
        if step > 1:
            send_up = (send_up.astype(F32) + up.astype(F32)).astype(F16)
            send_down = (send_down.astype(F32) + down.astype(F32)).astype(F16)
        up = lax.ppermute(send_up, "patch", [(i, i + 1) for i in range(step)])
        down = lax.ppermute(send_down, "patch", [(3 - i, 2 - i) for i in range(step)])
    own = lax.dynamic_index_in_dim(near, (patch % 2) ^ core, 0, keepdims=False)
    total = own.astype(F32) + (up.astype(F32) + down.astype(F32))
    return (total * (1.0 / LIFT)).astype(BF16)


def sum_own_slab(features, weight, patches):
    me = lax.axis_index("patch")
    rows = features.shape[0] // patches
    parts = jnp.dot(features, weight, preferred_element_type=F32) * LIFT

    def mine(slab):
        slab = jnp.clip(slab, 0, patches - 1)
        return lax.dynamic_slice_in_dim(parts, slab * rows, rows, 0)

    up = down = None
    for step in range(1, patches):
        send_up = mine(patches - step + me)
        send_down = mine(step - patches + me)
        if step > 1:
            send_up = send_up + up.astype(F32)
            send_down = send_down + down.astype(F32)
        up = lax.ppermute(send_up.astype(F16), "patch", [(i, i + 1) for i in range(step)])
        down = lax.ppermute(
            send_down.astype(F16), "patch", [(patches - 1 - i, patches - 2 - i) for i in range(step)]
        )
    total = mine(me)
    if patches > 1:
        total = total + (up.astype(F32) + down.astype(F32))
    return (total * (1.0 / LIFT)).astype(BF16)


def attend_and_project(patches, heads, chips, chunks, place_ref, query_ref, stale_ref, fresh_ref, w_ref, *out_refs):
    *out_refs, sums = out_refs
    send_refs, keep_refs = out_refs[:chunks], out_refs[chunks:]
    me = place_ref[0]
    rows = query_ref.shape[0]
    width = w_ref.shape[1] // (2 * chips)
    scale = 1.0 / HEAD_DIM**0.5
    starts = [pl.multiple_of(lax.rem(me + j, patches) * rows, rows) for j in range(1, patches)]
    dims = (((1,), (1,)), ((), ()))
    mixed_heads = []
    for h in range(heads):
        columns = slice(h * HEAD_DIM, (h + 1) * HEAD_DIM)
        query = query_ref[:, columns]
        keys = [fresh_ref[0, :, columns]] + [stale_ref[0, pl.ds(start, rows), columns] for start in starts]
        values = [fresh_ref[1, :, columns]] + [stale_ref[1, pl.ds(start, rows), columns] for start in starts]
        scores = [lax.dot_general(query, key, dims, preferred_element_type=F32) * scale for key in keys]
        top = functools.reduce(jnp.maximum, [jnp.max(s, axis=-1, keepdims=True) for s in scores])
        total = mixed = None
        for s, value in zip(scores, values):
            expo = jnp.exp(s - top)
            count = jnp.sum(expo, axis=-1, keepdims=True)
            part = jnp.dot(expo.astype(BF16), value, preferred_element_type=F32)
            total = count if total is None else total + count
            mixed = part if mixed is None else mixed + part
        mixed_heads.append((mixed / total).astype(BF16))
    heads_out = jnp.concatenate(mixed_heads, axis=1) if heads > 1 else mixed_heads[0]
    product = jnp.dot(heads_out, w_ref[...], preferred_element_type=F32)

    @pl.when(pl.program_id(0) == 0)
    def _():
        sums[...] = product

    @pl.when(pl.program_id(0) > 0)
    def _():
        sums[...] += product

    @pl.when(pl.program_id(0) == pl.num_programs(0) - 1)
    def _():
        part = width // chunks
        for c in range(chunks):
            for j in range(chips):
                theirs = pl.multiple_of(place_ref[1 + j] * width + c * part, part)
                ours = pl.multiple_of(place_ref[1 + chips + j] * width + c * part, part)
                there = slice(j * part, (j + 1) * part)
                send_refs[c][:, there] = sums[:, pl.ds(theirs, part)].astype(BF16)
                keep_refs[c][:, there] = sums[:, pl.ds(ours, part)]


def attend(query, stale_kv, fresh_kv, w_out, patches, ranks):
    rows, depth = query.shape
    tokens, model = stale_kv.shape[1], w_out.shape[1]
    rank = lax.axis_index("tensor").astype(jnp.int32)
    core, chip, chips = rank % 2, rank // 2, ranks // 2
    width = model // ranks
    order = [(chip + hop) % chips for hop in range(1, chips)] + [chip]
    me = lax.axis_index("patch").astype(jnp.int32)
    place = jnp.stack([me] + [2 * c + 1 - core for c in order] + [2 * c + core for c in order])
    heads = 2 if depth % (2 * HEAD_DIM) == 0 else 1
    block = heads * HEAD_DIM
    chunks = 2 if width % (2 * 128) == 0 else 1
    part = width // chunks
    results = pl.pallas_call(
        functools.partial(attend_and_project, patches, heads, chips, chunks),
        out_shape=[jax.ShapeDtypeStruct((rows, chips * part), BF16)] * chunks
        + [jax.ShapeDtypeStruct((rows, chips * part), F32)] * chunks,
        grid_spec=pltpu.PrefetchScalarGridSpec(
            num_scalar_prefetch=1,
            grid=(depth // block,),
            in_specs=[
                pl.BlockSpec((rows, block), lambda h, p: (0, h)),
                pl.BlockSpec((2, tokens, block), lambda h, p: (0, 0, h)),
                pl.BlockSpec((2, rows, block), lambda h, p: (0, 0, h)),
                pl.BlockSpec((block, model), lambda h, p: (h, 0)),
            ],
            out_specs=[pl.BlockSpec((rows, chips * part), lambda h, p: (0, 0))] * (2 * chunks),
            scratch_shapes=[pltpu.VMEM((rows, model), F32)],
        ),
        compiler_params=pltpu.CompilerParams(vmem_limit_bytes=48 * 2**20),
        cost_estimate=pl.CostEstimate(
            flops=4 * rows * tokens * depth + 2 * rows * depth * model,
            bytes_accessed=4 * tokens * depth + 2 * depth * model + 6 * rows * chips * width,
            transcendentals=rows * tokens * (depth // HEAD_DIM),
        ),
    )(place, query, stale_kv, fresh_kv, w_out)
    across = [(r, r ^ 1) for r in range(ranks)]
    got = [lax.ppermute(send, "tensor", across) for send in results[:chunks]]
    pieces = []
    for mine, theirs in zip(results[chunks:], got):

        def summed(j):
            return mine[:, j * part : (j + 1) * part] + theirs[:, j * part : (j + 1) * part].astype(F32)

        arrived = []
        for hop in range(1, chips):
            pairs = [(r, (r + 2 * hop) % ranks) for r in range(ranks)]
            arrived.append(lax.ppermute(summed(hop - 1).astype(BF16), "tensor", pairs))
        total = summed(chips - 1)
        for piece in arrived:
            total = total + piece.astype(F32)
        pieces.append(total.astype(BF16))
    return jnp.concatenate(pieces, axis=1)


def make_shards(patches, ranks):
    def shards(hidden_in, w_query, w_key, w_value, w_out, stale_kv):
        rows = hidden_in.shape[0]
        me = lax.axis_index("patch")
        own_stale = lax.dynamic_slice_in_dim(stale_kv, me * rows, rows, 1).astype(F32)
        w_both = jnp.concatenate([w_key, w_value], axis=1)
        if patches == ranks == 4:
            far, near = spread_in_pairs(hidden_in)
            both = sum_in_pairs(far, near, w_both)
            query = sum_in_pairs(far, near, w_query)
        else:
            features = spread_features(hidden_in)
            both = sum_own_slab(features, w_both, patches)
            query = sum_own_slab(features, w_query, patches)
        width = w_key.shape[1]
        fresh = lax.reduce_precision(both.astype(F32), 8, 7)
        fresh = jnp.stack([fresh[:, :width], fresh[:, width:]])
        delta = lax.reduce_precision(fresh - own_stale, 8, 7)
        own_new = (own_stale + delta).astype(BF16)
        sent, _ = lax.optimization_barrier((own_new, query))
        refreshed = lax.all_gather(sent, "patch", axis=1, tiled=True)
        attended = attend(query, stale_kv, own_new, w_out, patches, ranks)
        return (attended, refreshed)

    return shards


def solution(mesh):
    in_specs = (
        P(("groups", "patch"), "tensor"),
        P("patch", "tensor"),
        P("patch", "tensor"),
        P("patch", "tensor"),
        P("tensor", None),
        P(None, "groups", "tensor"),
    )
    out_specs = (P(("groups", "patch"), "tensor"), P(None, "groups", "tensor"))
    return jax.shard_map(
        make_shards(mesh.shape["patch"], mesh.shape["tensor"]),
        mesh=mesh,
        in_specs=in_specs,
        out_specs=out_specs,
        check_vma=False,
    )
```

```python
import functools

import jax
import jax.numpy as jnp
from jax import lax
from jax.experimental import pallas as pl
from jax.experimental.pallas import tpu as pltpu
from jax.sharding import PartitionSpec as P

HEAD_DIM = 128
F32 = jnp.float32
BF16 = jnp.bfloat16
F16 = jnp.float16
LIFT = 8.0


def spread_features(hidden):
    features = lax.all_gather(hidden, "tensor", axis=1, tiled=True)
    return lax.all_to_all(features, "patch", split_axis=1, concat_axis=0, tiled=True)


def after(value, *earlier):
    return lax.optimization_barrier((value, *earlier))[0] if earlier else value


def spread_in_pairs(hidden):
    rank, patch = lax.axis_index("tensor"), lax.axis_index("patch")
    core, chip = rank % 2, rank // 2

    def spread(slab_of, to_core, *earlier):
        along = [(4 * slab_of(z) + z, 4 * z + 2 * (z // 2) + to_core) for z in range(4)]
        here = lax.ppermute(after(hidden, *earlier), ("patch", "tensor"), along)
        across = [
            (4 * z + 2 * (z // 2) + to_core, 4 * z + 2 * (1 - z // 2) + to_core) for z in range(4)
        ]
        there = lax.ppermute(here, ("patch", "tensor"), across)
        block = jnp.where(chip == patch // 2, here, there)
        swap = [(4 * z + 2 * x + to_core, 4 * z + 2 * x + 1 - to_core) for z in range(4) for x in range(2)]
        other = lax.ppermute(block, ("patch", "tensor"), swap)
        return jnp.where(core == to_core, block, other), here

    outermost, here = spread(lambda z: 3 if z < 2 else 0, 0)
    inner, here = spread(lambda z: 2 if z < 2 else 1, 1, here)
    mate, here = spread(lambda z: z ^ 1, 0, here)
    own, _ = spread(lambda z: z, 1, here)
    return outermost, inner, mate, own


def sum_in_pairs(blocks, weight):
    patch = lax.axis_index("patch")
    is_end = (patch == 0) | (patch == 3)

    def project(features):
        return (jnp.dot(features, weight, preferred_element_type=F32) * LIFT).astype(F16)

    def plus(part, got):
        return (part.astype(F32) + got.astype(F32)).astype(F16)

    outermost, inner, mate, own = (lax.optimization_barrier(project(block)) for block in blocks)
    first = lax.ppermute(outermost, "patch", [(0, 1), (3, 2)])
    second = jnp.where(is_end, inner, plus(outermost, first))
    up = lax.ppermute(second, "patch", [(0, 1), (1, 2)])
    down = lax.ppermute(second, "patch", [(3, 2), (2, 1)])
    third_up = plus(jnp.where(patch == 1, inner, mate), up)
    third_down = plus(jnp.where(patch == 2, inner, mate), down)
    up = lax.ppermute(third_up, "patch", [(0, 1), (1, 2), (2, 3)])
    down = lax.ppermute(third_down, "patch", [(3, 2), (2, 1), (1, 0)])
    total = own.astype(F32) + (up.astype(F32) + down.astype(F32))
    return (total * (1.0 / LIFT)).astype(BF16)


def sum_own_slab(features, weight, patches):
    me = lax.axis_index("patch")
    rows = features.shape[0] // patches
    parts = jnp.dot(features, weight, preferred_element_type=F32) * LIFT

    def mine(slab):
        slab = jnp.clip(slab, 0, patches - 1)
        return lax.dynamic_slice_in_dim(parts, slab * rows, rows, 0)

    up = down = None
    for step in range(1, patches):
        send_up = mine(patches - step + me)
        send_down = mine(step - patches + me)
        if step > 1:
            send_up = send_up + up.astype(F32)
            send_down = send_down + down.astype(F32)
        up = lax.ppermute(send_up.astype(F16), "patch", [(i, i + 1) for i in range(step)])
        down = lax.ppermute(
            send_down.astype(F16), "patch", [(patches - 1 - i, patches - 2 - i) for i in range(step)]
        )
    total = mine(me)
    if patches > 1:
        total = total + (up.astype(F32) + down.astype(F32))
    return (total * (1.0 / LIFT)).astype(BF16)


def attend_and_project(patches, heads, chips, chunks, place_ref, query_ref, stale_ref, fresh_ref, w_ref, *out_refs):
    *out_refs, sums = out_refs
    send_refs, keep_refs = out_refs[:chunks], out_refs[chunks:]
    me = place_ref[0]
    rows = query_ref.shape[0]
    width = w_ref.shape[1] // (2 * chips)
    scale = 1.0 / HEAD_DIM**0.5
    starts = [pl.multiple_of(lax.rem(me + j, patches) * rows, rows) for j in range(1, patches)]
    dims = (((1,), (1,)), ((), ()))
    mixed_heads = []
    for h in range(heads):
        columns = slice(h * HEAD_DIM, (h + 1) * HEAD_DIM)
        query = query_ref[:, columns]
        keys = [fresh_ref[0, :, columns]] + [stale_ref[0, pl.ds(start, rows), columns] for start in starts]
        values = [fresh_ref[1, :, columns]] + [stale_ref[1, pl.ds(start, rows), columns] for start in starts]
        scores = [lax.dot_general(query, key, dims, preferred_element_type=F32) * scale for key in keys]
        top = functools.reduce(jnp.maximum, [jnp.max(s, axis=-1, keepdims=True) for s in scores])
        total = mixed = None
        for s, value in zip(scores, values):
            expo = jnp.exp(s - top)
            count = jnp.sum(expo, axis=-1, keepdims=True)
            part = jnp.dot(expo.astype(BF16), value, preferred_element_type=F32)
            total = count if total is None else total + count
            mixed = part if mixed is None else mixed + part
        mixed_heads.append((mixed / total).astype(BF16))
    heads_out = jnp.concatenate(mixed_heads, axis=1) if heads > 1 else mixed_heads[0]
    product = jnp.dot(heads_out, w_ref[...], preferred_element_type=F32)

    @pl.when(pl.program_id(0) == 0)
    def _():
        sums[...] = product

    @pl.when(pl.program_id(0) > 0)
    def _():
        sums[...] += product

    @pl.when(pl.program_id(0) == pl.num_programs(0) - 1)
    def _():
        part = width // chunks
        for c in range(chunks):
            for j in range(chips):
                theirs = pl.multiple_of(place_ref[1 + j] * width + c * part, part)
                ours = pl.multiple_of(place_ref[1 + chips + j] * width + c * part, part)
                there = slice(j * part, (j + 1) * part)
                send_refs[c][:, there] = sums[:, pl.ds(theirs, part)].astype(BF16)
                keep_refs[c][:, there] = sums[:, pl.ds(ours, part)]


def attend(query, stale_kv, fresh_kv, w_out, patches, ranks):
    rows, depth = query.shape
    tokens, model = stale_kv.shape[1], w_out.shape[1]
    rank = lax.axis_index("tensor").astype(jnp.int32)
    core, chip, chips = rank % 2, rank // 2, ranks // 2
    width = model // ranks
    order = [(chip + hop) % chips for hop in range(1, chips)] + [chip]
    me = lax.axis_index("patch").astype(jnp.int32)
    place = jnp.stack([me] + [2 * c + 1 - core for c in order] + [2 * c + core for c in order])
    heads = 2 if depth % (2 * HEAD_DIM) == 0 else 1
    block = heads * HEAD_DIM
    chunks = 2 if width % (2 * 128) == 0 else 1
    part = width // chunks
    results = pl.pallas_call(
        functools.partial(attend_and_project, patches, heads, chips, chunks),
        out_shape=[jax.ShapeDtypeStruct((rows, chips * part), BF16)] * chunks
        + [jax.ShapeDtypeStruct((rows, chips * part), F32)] * chunks,
        grid_spec=pltpu.PrefetchScalarGridSpec(
            num_scalar_prefetch=1,
            grid=(depth // block,),
            in_specs=[
                pl.BlockSpec((rows, block), lambda h, p: (0, h)),
                pl.BlockSpec((2, tokens, block), lambda h, p: (0, 0, h)),
                pl.BlockSpec((2, rows, block), lambda h, p: (0, 0, h)),
                pl.BlockSpec((block, model), lambda h, p: (h, 0)),
            ],
            out_specs=[pl.BlockSpec((rows, chips * part), lambda h, p: (0, 0))] * (2 * chunks),
            scratch_shapes=[pltpu.VMEM((rows, model), F32)],
        ),
        compiler_params=pltpu.CompilerParams(vmem_limit_bytes=48 * 2**20),
        cost_estimate=pl.CostEstimate(
            flops=4 * rows * tokens * depth + 2 * rows * depth * model,
            bytes_accessed=4 * tokens * depth + 2 * depth * model + 6 * rows * chips * width,
            transcendentals=rows * tokens * (depth // HEAD_DIM),
        ),
    )(place, query, stale_kv, fresh_kv, w_out)
    across = [(r, r ^ 1) for r in range(ranks)]
    got = [lax.ppermute(send, "tensor", across) for send in results[:chunks]]
    pieces = []
    for mine, theirs in zip(results[chunks:], got):

        def summed(j):
            return mine[:, j * part : (j + 1) * part] + theirs[:, j * part : (j + 1) * part].astype(F32)

        arrived = []
        for hop in range(1, chips):
            pairs = [(r, (r + 2 * hop) % ranks) for r in range(ranks)]
            arrived.append(lax.ppermute(summed(hop - 1).astype(BF16), "tensor", pairs))
        total = summed(chips - 1)
        for piece in arrived:
            total = total + piece.astype(F32)
        pieces.append(total.astype(BF16))
    return jnp.concatenate(pieces, axis=1)


def make_shards(patches, ranks):
    def shards(hidden_in, w_query, w_key, w_value, w_out, stale_kv):
        rows = hidden_in.shape[0]
        me = lax.axis_index("patch")
        own_stale = lax.dynamic_slice_in_dim(stale_kv, me * rows, rows, 1).astype(F32)
        w_both = jnp.concatenate([w_key, w_value], axis=1)
        if patches == ranks == 4:
            blocks = spread_in_pairs(hidden_in)
            both = sum_in_pairs(blocks, w_both)
            query = sum_in_pairs(blocks, w_query)
        else:
            features = spread_features(hidden_in)
            both = sum_own_slab(features, w_both, patches)
            query = sum_own_slab(features, w_query, patches)
        width = w_key.shape[1]
        fresh = lax.reduce_precision(both.astype(F32), 8, 7)
        fresh = jnp.stack([fresh[:, :width], fresh[:, width:]])
        delta = lax.reduce_precision(fresh - own_stale, 8, 7)
        own_new = (own_stale + delta).astype(BF16)
        refreshed = lax.all_gather(after(own_new, query), "patch", axis=1, tiled=True)
        attended = attend(query, stale_kv, own_new, w_out, patches, ranks)
        return (attended, refreshed)

    return shards


def solution(mesh):
    in_specs = (
        P(("groups", "patch"), "tensor"),
        P("patch", "tensor"),
        P("patch", "tensor"),
        P("patch", "tensor"),
        P("tensor", None),
        P(None, "groups", "tensor"),
    )
    out_specs = (P(("groups", "patch"), "tensor"), P(None, "groups", "tensor"))
    return jax.shard_map(
        make_shards(mesh.shape["patch"], mesh.shape["tensor"]),
        mesh=mesh,
        in_specs=in_specs,
        out_specs=out_specs,
        check_vma=False,
    )
```

```python
import functools

import jax
import jax.numpy as jnp
from jax import lax
from jax.experimental import pallas as pl
from jax.experimental.pallas import tpu as pltpu
from jax.sharding import PartitionSpec as P

HEAD_DIM = 128
F32 = jnp.float32
BF16 = jnp.bfloat16
F16 = jnp.float16
LIFT = 8.0


def spread_features(hidden):
    features = lax.all_gather(hidden, "tensor", axis=1, tiled=True)
    return lax.all_to_all(features, "patch", split_axis=1, concat_axis=0, tiled=True)


def after(value, *earlier):
    return lax.optimization_barrier((value, *earlier))[0] if earlier else value


def spread_in_pairs(hidden):
    rank, patch = lax.axis_index("tensor"), lax.axis_index("patch")
    half = hidden.shape[0] // 2
    across = [(r, r ^ 2) for r in range(4)]
    straight = hidden[:half]
    crossing = lax.ppermute(hidden[half:], "tensor", across)
    is_straight = patch // 2 == rank // 2

    def along(block, flip, far):
        pairs = [
            (4 * s + r, 4 * (r ^ flip) + 2 * (r // 2) + s % 2)
            for s in range(4)
            for r in range(4)
            if ((r ^ flip) // 2 != s // 2) == far
        ]
        return lax.ppermute(block, ("patch", "tensor"), pairs)

    def both_slabs(far):
        held = jnp.where(is_straight, along(straight, 0, far), along(crossing, 2, far))
        other = lax.ppermute(held, "tensor", across)
        low = jnp.where(is_straight, held, other)
        high = jnp.where(is_straight, other, held)
        mine = jnp.concatenate([low, high])
        theirs = lax.ppermute(mine, "tensor", [(r, r ^ 1) for r in range(4)])
        return jnp.concatenate([mine, theirs])

    return both_slabs(True), both_slabs(False)


def sum_in_pairs(far, near, weight):
    patch, core = lax.axis_index("patch"), lax.axis_index("tensor") % 2
    is_end = (patch == 0) | (patch == 3)

    def project(features):
        product = (jnp.dot(features, weight, preferred_element_type=F32) * LIFT).astype(F16)
        return product.reshape(2, features.shape[0] // 2, weight.shape[1])

    def slab(pair, odd):
        return lax.dynamic_index_in_dim(pair, odd ^ core, 0, keepdims=False)

    def plus(part, got):
        return (part.astype(F32) + got.astype(F32)).astype(F16)

    far, near = project(far), lax.optimization_barrier(project(near))
    outermost, inner = slab(far, 1 - patch // 2), slab(far, patch // 2)
    own, mate = slab(near, patch % 2), slab(near, 1 - patch % 2)
    first = lax.ppermute(outermost, "patch", [(0, 1), (3, 2)])
    second = jnp.where(is_end, inner, plus(outermost, first))
    up = lax.ppermute(second, "patch", [(0, 1), (1, 2)])
    down = lax.ppermute(second, "patch", [(3, 2), (2, 1)])
    third_up = plus(jnp.where(patch == 1, inner, mate), up)
    third_down = plus(jnp.where(patch == 2, inner, mate), down)
    up = lax.ppermute(third_up, "patch", [(0, 1), (1, 2), (2, 3)])
    down = lax.ppermute(third_down, "patch", [(3, 2), (2, 1), (1, 0)])
    total = own.astype(F32) + (up.astype(F32) + down.astype(F32))
    return (total * (1.0 / LIFT)).astype(BF16)


class PairGather:
    def __init__(self, own):
        self.own = own
        self.mate = lax.ppermute(own, "patch", [(0, 1), (1, 0), (2, 3), (3, 2)])
        self.across = lax.ppermute(own, "patch", [(1, 2), (2, 1)])

    def into(self, whole, index, *earlier):
        patch = lax.axis_index("patch")
        rows = self.own.shape[0]
        is_inner = (patch == 1) | (patch == 2)
        outward = [(1, 0), (2, 3)]
        across_mate = lax.ppermute(self.mate, "patch", [(1, 2), (2, 1)])
        far_inner = jnp.where(is_inner, self.across, lax.ppermute(self.across, "patch", outward))
        last = lax.ppermute(after(across_mate, *earlier), "patch", outward)
        far_outer = jnp.where(is_inner, across_mate, last)
        low = patch < 2
        slabs = (patch, patch ^ 1, jnp.where(low, 2, 1), jnp.where(low, 3, 0))
        for slab, block in zip(slabs, (self.own, self.mate, far_inner, far_outer)):
            whole = lax.dynamic_update_slice(whole, block[None], (index, slab * rows, 0))
        return whole


def sum_own_slab(features, weight, patches):
    me = lax.axis_index("patch")
    rows = features.shape[0] // patches
    parts = jnp.dot(features, weight, preferred_element_type=F32) * LIFT

    def mine(slab):
        slab = jnp.clip(slab, 0, patches - 1)
        return lax.dynamic_slice_in_dim(parts, slab * rows, rows, 0)

    up = down = None
    for step in range(1, patches):
        send_up = mine(patches - step + me)
        send_down = mine(step - patches + me)
        if step > 1:
            send_up = send_up + up.astype(F32)
            send_down = send_down + down.astype(F32)
        up = lax.ppermute(send_up.astype(F16), "patch", [(i, i + 1) for i in range(step)])
        down = lax.ppermute(
            send_down.astype(F16), "patch", [(patches - 1 - i, patches - 2 - i) for i in range(step)]
        )
    total = mine(me)
    if patches > 1:
        total = total + (up.astype(F32) + down.astype(F32))
    return (total * (1.0 / LIFT)).astype(BF16)


def attend_and_project(patches, heads, chips, chunks, place_ref, query_ref, stale_ref, key_ref, value_ref, w_ref, *out_refs):
    *out_refs, sums = out_refs
    send_refs, keep_refs = out_refs[:chunks], out_refs[chunks:]
    me = place_ref[0]
    rows = query_ref.shape[0]
    width = w_ref.shape[1] // (2 * chips)
    scale = 1.0 / HEAD_DIM**0.5
    starts = [pl.multiple_of(lax.rem(me + j, patches) * rows, rows) for j in range(1, patches)]
    dims = (((1,), (1,)), ((), ()))
    mixed_heads = []
    for h in range(heads):
        columns = slice(h * HEAD_DIM, (h + 1) * HEAD_DIM)
        query = query_ref[:, columns]
        keys = [key_ref[:, columns]] + [stale_ref[0, pl.ds(start, rows), columns] for start in starts]
        values = [value_ref[:, columns]] + [stale_ref[1, pl.ds(start, rows), columns] for start in starts]
        scores = [lax.dot_general(query, key, dims, preferred_element_type=F32) * scale for key in keys]
        top = functools.reduce(jnp.maximum, [jnp.max(s, axis=-1, keepdims=True) for s in scores])
        total = mixed = None
        for s, value in zip(scores, values):
            expo = jnp.exp(s - top)
            count = jnp.sum(expo, axis=-1, keepdims=True)
            part = jnp.dot(expo.astype(BF16), value, preferred_element_type=F32)
            total = count if total is None else total + count
            mixed = part if mixed is None else mixed + part
        mixed_heads.append((mixed / total).astype(BF16))
    heads_out = jnp.concatenate(mixed_heads, axis=1) if heads > 1 else mixed_heads[0]
    product = jnp.dot(heads_out, w_ref[...], preferred_element_type=F32)

    @pl.when(pl.program_id(0) == 0)
    def _():
        sums[...] = product

    @pl.when(pl.program_id(0) > 0)
    def _():
        sums[...] += product

    @pl.when(pl.program_id(0) == pl.num_programs(0) - 1)
    def _():
        part = width // chunks
        for c in range(chunks):
            for j in range(chips):
                theirs = pl.multiple_of(place_ref[1 + j] * width + c * part, part)
                ours = pl.multiple_of(place_ref[1 + chips + j] * width + c * part, part)
                there = slice(j * part, (j + 1) * part)
                send_refs[c][:, there] = sums[:, pl.ds(theirs, part)].astype(BF16)
                keep_refs[c][:, there] = sums[:, pl.ds(ours, part)]


def attend(query, stale_kv, key_new, value_new, w_out, patches, ranks):
    rows, depth = query.shape
    tokens, model = stale_kv.shape[1], w_out.shape[1]
    rank = lax.axis_index("tensor").astype(jnp.int32)
    core, chip, chips = rank % 2, rank // 2, ranks // 2
    width = model // ranks
    order = [(chip + hop) % chips for hop in range(1, chips)] + [chip]
    me = lax.axis_index("patch").astype(jnp.int32)
    place = jnp.stack([me] + [2 * c + 1 - core for c in order] + [2 * c + core for c in order])
    heads = 2 if depth % (2 * HEAD_DIM) == 0 else 1
    block = heads * HEAD_DIM
    chunks = 2 if width % (2 * 128) == 0 else 1
    part = width // chunks
    results = pl.pallas_call(
        functools.partial(attend_and_project, patches, heads, chips, chunks),
        out_shape=[jax.ShapeDtypeStruct((rows, chips * part), BF16)] * chunks
        + [jax.ShapeDtypeStruct((rows, chips * part), F32)] * chunks,
        grid_spec=pltpu.PrefetchScalarGridSpec(
            num_scalar_prefetch=1,
            grid=(depth // block,),
            in_specs=[
                pl.BlockSpec((rows, block), lambda h, p: (0, h)),
                pl.BlockSpec((2, tokens, block), lambda h, p: (0, 0, h)),
                pl.BlockSpec((rows, block), lambda h, p: (0, h)),
                pl.BlockSpec((rows, block), lambda h, p: (0, h)),
                pl.BlockSpec((block, model), lambda h, p: (h, 0)),
            ],
            out_specs=[pl.BlockSpec((rows, chips * part), lambda h, p: (0, 0))] * (2 * chunks),
            scratch_shapes=[pltpu.VMEM((rows, model), F32)],
        ),
        compiler_params=pltpu.CompilerParams(vmem_limit_bytes=48 * 2**20),
        cost_estimate=pl.CostEstimate(
            flops=4 * rows * tokens * depth + 2 * rows * depth * model,
            bytes_accessed=4 * tokens * depth + 2 * depth * model + 6 * rows * chips * width,
            transcendentals=rows * tokens * (depth // HEAD_DIM),
        ),
    )(place, query, stale_kv, key_new, value_new, w_out)
    across = [(r, r ^ 1) for r in range(ranks)]
    got = [lax.ppermute(send, "tensor", across) for send in results[:chunks]]
    pieces, sends = [], []
    for mine, theirs in zip(results[chunks:], got):

        def summed(j):
            return mine[:, j * part : (j + 1) * part] + theirs[:, j * part : (j + 1) * part].astype(F32)

        arrived = []
        for hop in range(1, chips):
            pairs = [(r, (r + 2 * hop) % ranks) for r in range(ranks)]
            sends.append(summed(hop - 1).astype(BF16))
            arrived.append(lax.ppermute(sends[-1], "tensor", pairs))
        total = summed(chips - 1)
        for piece in arrived:
            total = total + piece.astype(F32)
        pieces.append(total.astype(BF16))
    return jnp.concatenate(pieces, axis=1), sends


def make_shards(patches, ranks):
    def shards(hidden_in, w_query, w_key, w_value, w_out, stale_kv):
        rows = hidden_in.shape[0]
        me = lax.axis_index("patch")
        own_stale = lax.dynamic_slice_in_dim(stale_kv, me * rows, rows, 1)
        in_pairs = patches == ranks == 4
        w_both = jnp.concatenate([w_key, w_value], axis=1)
        if in_pairs:
            far, near = spread_in_pairs(hidden_in)
            both = sum_in_pairs(far, near, w_both)
            query = sum_in_pairs(far, near, w_query)
        else:
            features = spread_features(hidden_in)
            both = sum_own_slab(features, w_both, patches)
            query = sum_own_slab(features, w_query, patches)

        def refresh(fresh, stale):
            fresh = lax.reduce_precision(fresh.astype(F32), 8, 7)
            stale = stale.astype(F32)
            return (stale + lax.reduce_precision(fresh - stale, 8, 7)).astype(BF16)

        width = w_key.shape[1]
        key_new = refresh(both[:, :width], own_stale[0])
        value_new = refresh(both[:, width:], own_stale[1])
        if in_pairs:
            keys, values = PairGather(after(key_new, query)), PairGather(after(value_new, query))
            query = after(query, keys.mate, keys.across)
        attended, sent = attend(query, stale_kv, key_new, value_new, w_out, patches, ranks)
        if in_pairs:
            refreshed = keys.into(jnp.zeros_like(stale_kv), 0, *sent)
            refreshed = values.into(refreshed, 1, *sent)
        else:
            refreshed = lax.all_gather(jnp.stack([key_new, value_new]), "patch", axis=1, tiled=True)
        return (attended, refreshed)

    return shards


def solution(mesh):
    in_specs = (
        P(("groups", "patch"), "tensor"),
        P("patch", "tensor"),
        P("patch", "tensor"),
        P("patch", "tensor"),
        P("tensor", None),
        P(None, "groups", "tensor"),
    )
    out_specs = (P(("groups", "patch"), "tensor"), P(None, "groups", "tensor"))
    return jax.shard_map(
        make_shards(mesh.shape["patch"], mesh.shape["tensor"]),
        mesh=mesh,
        in_specs=in_specs,
        out_specs=out_specs,
        check_vma=False,
    )
```

```python
import functools

import jax
import jax.numpy as jnp
from jax import lax
from jax.experimental import pallas as pl
from jax.experimental.pallas import tpu as pltpu
from jax.sharding import PartitionSpec as P

HEAD_DIM = 128
F32 = jnp.float32
BF16 = jnp.bfloat16
F16 = jnp.float16
LIFT = 8.0


def spread_features(hidden):
    features = lax.all_gather(hidden, "tensor", axis=1, tiled=True)
    return lax.all_to_all(features, "patch", split_axis=1, concat_axis=0, tiled=True)


def after(value, *earlier):
    return lax.optimization_barrier((value, *earlier))[0] if earlier else value


def spread_in_pairs(hidden):
    rank, patch = lax.axis_index("tensor"), lax.axis_index("patch")
    half = hidden.shape[0] // 2
    across = [(r, r ^ 2) for r in range(4)]
    straight = hidden[:half]
    crossing = lax.ppermute(hidden[half:], "tensor", across)
    is_straight = patch // 2 == rank // 2

    def along(block, flip, far):
        pairs = [
            (4 * s + r, 4 * (r ^ flip) + 2 * (r // 2) + s % 2)
            for s in range(4)
            for r in range(4)
            if ((r ^ flip) // 2 != s // 2) == far
        ]
        return lax.ppermute(block, ("patch", "tensor"), pairs)

    def both_slabs(far):
        held = jnp.where(is_straight, along(straight, 0, far), along(crossing, 2, far))
        other = lax.ppermute(held, "tensor", across)
        low = jnp.where(is_straight, held, other)
        high = jnp.where(is_straight, other, held)
        mine = jnp.concatenate([low, high])
        theirs = lax.ppermute(mine, "tensor", [(r, r ^ 1) for r in range(4)])
        return jnp.concatenate([mine, theirs])

    return both_slabs(True), both_slabs(False)


def sum_in_pairs(far, near, weight):
    patch, core = lax.axis_index("patch"), lax.axis_index("tensor") % 2
    is_end = (patch == 0) | (patch == 3)

    def project(features):
        product = (jnp.dot(features, weight, preferred_element_type=F32) * LIFT).astype(F16)
        return product.reshape(2, features.shape[0] // 2, weight.shape[1])

    def slab(pair, odd):
        return lax.dynamic_index_in_dim(pair, odd ^ core, 0, keepdims=False)

    def plus(part, got):
        return (part.astype(F32) + got.astype(F32)).astype(F16)

    far, near = project(far), lax.optimization_barrier(project(near))
    outermost, inner = slab(far, 1 - patch // 2), slab(far, patch // 2)
    own, mate = slab(near, patch % 2), slab(near, 1 - patch % 2)
    first = lax.ppermute(outermost, "patch", [(0, 1), (3, 2)])
    second = jnp.where(is_end, inner, plus(outermost, first))
    up = lax.ppermute(second, "patch", [(0, 1), (1, 2)])
    down = lax.ppermute(second, "patch", [(3, 2), (2, 1)])
    third_up = plus(jnp.where(patch == 1, inner, mate), up)
    third_down = plus(jnp.where(patch == 2, inner, mate), down)
    up = lax.ppermute(third_up, "patch", [(0, 1), (1, 2), (2, 3)])
    down = lax.ppermute(third_down, "patch", [(3, 2), (2, 1), (1, 0)])
    total = own.astype(F32) + (up.astype(F32) + down.astype(F32))
    return (total * (1.0 / LIFT)).astype(BF16)


class PairGather:
    def __init__(self, own):
        self.own = own
        self.mate = lax.ppermute(own, "patch", [(0, 1), (1, 0), (2, 3), (3, 2)])
        self.across = lax.ppermute(own, "patch", [(1, 2), (2, 1)])

    def into(self, whole, index, *earlier):
        patch = lax.axis_index("patch")
        rows = self.own.shape[0]
        is_inner = (patch == 1) | (patch == 2)
        outward = [(1, 0), (2, 3)]
        across_mate = lax.ppermute(self.mate, "patch", [(1, 2), (2, 1)])
        far_inner = jnp.where(is_inner, self.across, lax.ppermute(self.across, "patch", outward))
        last = lax.ppermute(after(across_mate, *earlier), "patch", outward)
        far_outer = jnp.where(is_inner, across_mate, last)
        low = patch < 2
        slabs = (patch, patch ^ 1, jnp.where(low, 2, 1), jnp.where(low, 3, 0))
        for slab, block in zip(slabs, (self.own, self.mate, far_inner, far_outer)):
            whole = lax.dynamic_update_slice(whole, block[None], (index, slab * rows, 0))
        return whole


def sum_own_slab(features, weight, patches):
    me = lax.axis_index("patch")
    rows = features.shape[0] // patches
    parts = jnp.dot(features, weight, preferred_element_type=F32) * LIFT

    def mine(slab):
        slab = jnp.clip(slab, 0, patches - 1)
        return lax.dynamic_slice_in_dim(parts, slab * rows, rows, 0)

    up = down = None
    for step in range(1, patches):
        send_up = mine(patches - step + me)
        send_down = mine(step - patches + me)
        if step > 1:
            send_up = send_up + up.astype(F32)
            send_down = send_down + down.astype(F32)
        up = lax.ppermute(send_up.astype(F16), "patch", [(i, i + 1) for i in range(step)])
        down = lax.ppermute(
            send_down.astype(F16), "patch", [(patches - 1 - i, patches - 2 - i) for i in range(step)]
        )
    total = mine(me)
    if patches > 1:
        total = total + (up.astype(F32) + down.astype(F32))
    return (total * (1.0 / LIFT)).astype(BF16)


def attend_and_project(patches, heads, chips, chunks, place_ref, query_ref, stale_ref, key_ref, value_ref, w_ref, *out_refs):
    *out_refs, sums = out_refs
    send_refs, keep_refs = out_refs[:chunks], out_refs[chunks:]
    me = place_ref[0]
    rows = query_ref.shape[0]
    width = w_ref.shape[1] // (2 * chips)
    scale = 1.0 / HEAD_DIM**0.5
    starts = [pl.multiple_of(lax.rem(me + j, patches) * rows, rows) for j in range(1, patches)]
    dims = (((1,), (1,)), ((), ()))
    mixed_heads = []
    for h in range(heads):
        columns = slice(h * HEAD_DIM, (h + 1) * HEAD_DIM)
        query = query_ref[:, columns]
        keys = [key_ref[:, columns]] + [stale_ref[0, pl.ds(start, rows), columns] for start in starts]
        values = [value_ref[:, columns]] + [stale_ref[1, pl.ds(start, rows), columns] for start in starts]
        scores = [lax.dot_general(query, key, dims, preferred_element_type=F32) * scale for key in keys]
        top = functools.reduce(jnp.maximum, [jnp.max(s, axis=-1, keepdims=True) for s in scores])
        total = mixed = None
        for s, value in zip(scores, values):
            expo = jnp.exp(s - top)
            count = jnp.sum(expo, axis=-1, keepdims=True)
            part = jnp.dot(expo.astype(BF16), value, preferred_element_type=F32)
            total = count if total is None else total + count
            mixed = part if mixed is None else mixed + part
        mixed_heads.append((mixed / total).astype(BF16))
    heads_out = jnp.concatenate(mixed_heads, axis=1) if heads > 1 else mixed_heads[0]
    product = jnp.dot(heads_out, w_ref[...], preferred_element_type=F32)

    @pl.when(pl.program_id(0) == 0)
    def _():
        sums[...] = product

    @pl.when(pl.program_id(0) > 0)
    def _():
        sums[...] += product

    @pl.when(pl.program_id(0) == pl.num_programs(0) - 1)
    def _():
        part = width // chunks
        for c in range(chunks):
            for j in range(chips):
                theirs = pl.multiple_of(place_ref[1 + j] * width + c * part, part)
                ours = pl.multiple_of(place_ref[1 + chips + j] * width + c * part, part)
                there = slice(j * part, (j + 1) * part)
                send_refs[c][:, there] = sums[:, pl.ds(theirs, part)].astype(BF16)
                keep_refs[c][:, there] = sums[:, pl.ds(ours, part)]


def attend(query, stale_kv, key_new, value_new, w_out, patches, ranks, *earlier):
    rows, depth = query.shape
    tokens, model = stale_kv.shape[1], w_out.shape[1]
    rank = lax.axis_index("tensor").astype(jnp.int32)
    core, chip, chips = rank % 2, rank // 2, ranks // 2
    width = model // ranks
    order = [(chip + hop) % chips for hop in range(1, chips)] + [chip]
    me = lax.axis_index("patch").astype(jnp.int32)
    place = jnp.stack([me] + [2 * c + 1 - core for c in order] + [2 * c + core for c in order])
    heads = 2 if depth % (2 * HEAD_DIM) == 0 else 1
    block = heads * HEAD_DIM
    chunks = 2 if width % (2 * 128) == 0 else 1
    part = width // chunks
    results = pl.pallas_call(
        functools.partial(attend_and_project, patches, heads, chips, chunks),
        out_shape=[jax.ShapeDtypeStruct((rows, chips * part), BF16)] * chunks
        + [jax.ShapeDtypeStruct((rows, chips * part), F32)] * chunks,
        grid_spec=pltpu.PrefetchScalarGridSpec(
            num_scalar_prefetch=1,
            grid=(depth // block,),
            in_specs=[
                pl.BlockSpec((rows, block), lambda h, p: (0, h)),
                pl.BlockSpec((2, tokens, block), lambda h, p: (0, 0, h)),
                pl.BlockSpec((rows, block), lambda h, p: (0, h)),
                pl.BlockSpec((rows, block), lambda h, p: (0, h)),
                pl.BlockSpec((block, model), lambda h, p: (h, 0)),
            ],
            out_specs=[pl.BlockSpec((rows, chips * part), lambda h, p: (0, 0))] * (2 * chunks),
            scratch_shapes=[pltpu.VMEM((rows, model), F32)],
        ),
        compiler_params=pltpu.CompilerParams(vmem_limit_bytes=48 * 2**20),
        cost_estimate=pl.CostEstimate(
            flops=4 * rows * tokens * depth + 2 * rows * depth * model,
            bytes_accessed=4 * tokens * depth + 2 * depth * model + 6 * rows * chips * width,
            transcendentals=rows * tokens * (depth // HEAD_DIM),
        ),
    )(place, query, stale_kv, key_new, value_new, w_out)
    across = [(r, r ^ 1) for r in range(ranks)]
    got = [lax.ppermute(after(send, *earlier), "tensor", across) for send in results[:chunks]]
    pieces, sends = [], []
    for mine, theirs in zip(results[chunks:], got):

        def summed(j):
            return mine[:, j * part : (j + 1) * part] + theirs[:, j * part : (j + 1) * part].astype(F32)

        arrived = []
        for hop in range(1, chips):
            pairs = [(r, (r + 2 * hop) % ranks) for r in range(ranks)]
            sends.append(summed(hop - 1).astype(BF16))
            arrived.append(lax.ppermute(sends[-1], "tensor", pairs))
        total = summed(chips - 1)
        for piece in arrived:
            total = total + piece.astype(F32)
        pieces.append(total.astype(BF16))
    return jnp.concatenate(pieces, axis=1), sends


def make_shards(patches, ranks):
    def shards(hidden_in, w_query, w_key, w_value, w_out, stale_kv):
        rows = hidden_in.shape[0]
        me = lax.axis_index("patch")
        own_stale = lax.dynamic_slice_in_dim(stale_kv, me * rows, rows, 1)
        in_pairs = patches == ranks == 4
        w_both = jnp.concatenate([w_key, w_value], axis=1)
        if in_pairs:
            far, near = spread_in_pairs(hidden_in)
            both = sum_in_pairs(far, near, w_both)
            query = sum_in_pairs(far, near, w_query)
        else:
            features = spread_features(hidden_in)
            both = sum_own_slab(features, w_both, patches)
            query = sum_own_slab(features, w_query, patches)

        def refresh(fresh, stale):
            fresh = lax.reduce_precision(fresh.astype(F32), 8, 7)
            stale = stale.astype(F32)
            return (stale + lax.reduce_precision(fresh - stale, 8, 7)).astype(BF16)

        width = w_key.shape[1]
        key_new = refresh(both[:, :width], own_stale[0])
        value_new = refresh(both[:, width:], own_stale[1])
        if in_pairs:
            keys, values = PairGather(after(key_new, query)), PairGather(after(value_new, query))
            first_hop = (keys.mate, keys.across, values.mate, values.across)
        else:
            first_hop = ()
        attended, sent = attend(query, stale_kv, key_new, value_new, w_out, patches, ranks, *first_hop)
        if in_pairs:
            refreshed = keys.into(jnp.zeros_like(stale_kv), 0, *sent)
            refreshed = values.into(refreshed, 1, *sent)
        else:
            refreshed = lax.all_gather(jnp.stack([key_new, value_new]), "patch", axis=1, tiled=True)
        return (attended, refreshed)

    return shards


def solution(mesh):
    in_specs = (
        P(("groups", "patch"), "tensor"),
        P("patch", "tensor"),
        P("patch", "tensor"),
        P("patch", "tensor"),
        P("tensor", None),
        P(None, "groups", "tensor"),
    )
    out_specs = (P(("groups", "patch"), "tensor"), P(None, "groups", "tensor"))
    return jax.shard_map(
        make_shards(mesh.shape["patch"], mesh.shape["tensor"]),
        mesh=mesh,
        in_specs=in_specs,
        out_specs=out_specs,
        check_vma=False,
    )
```

```python
import functools

import jax
import jax.numpy as jnp
from jax import lax
from jax.experimental import pallas as pl
from jax.experimental.pallas import tpu as pltpu
from jax.sharding import PartitionSpec as P

HEAD_DIM = 128
F32 = jnp.float32
BF16 = jnp.bfloat16
F16 = jnp.float16
LIFT = 8.0


def spread_features(hidden):
    features = lax.all_gather(hidden, "tensor", axis=1, tiled=True)
    return lax.all_to_all(features, "patch", split_axis=1, concat_axis=0, tiled=True)


def after(value, *earlier):
    return lax.optimization_barrier((value, *earlier))[0] if earlier else value


def spread_in_pairs(hidden):
    rank, patch = lax.axis_index("tensor"), lax.axis_index("patch")
    half = hidden.shape[0] // 2
    across = [(r, r ^ 2) for r in range(4)]
    straight = hidden[:half]
    crossing = lax.ppermute(hidden[half:], "tensor", across)
    is_straight = patch // 2 == rank // 2

    def along(block, flip, far):
        pairs = [
            (4 * s + r, 4 * (r ^ flip) + 2 * (r // 2) + s % 2)
            for s in range(4)
            for r in range(4)
            if ((r ^ flip) // 2 != s // 2) == far
        ]
        return lax.ppermute(block, ("patch", "tensor"), pairs)

    def both_slabs(far):
        held = jnp.where(is_straight, along(straight, 0, far), along(crossing, 2, far))
        other = lax.ppermute(held, "tensor", across)
        low = jnp.where(is_straight, held, other)
        high = jnp.where(is_straight, other, held)
        mine = jnp.concatenate([low, high])
        theirs = lax.ppermute(mine, "tensor", [(r, r ^ 1) for r in range(4)])
        return jnp.concatenate([mine, theirs])

    return both_slabs(True), both_slabs(False)


def sum_in_pairs(far, near, weight):
    patch, core = lax.axis_index("patch"), lax.axis_index("tensor") % 2
    is_end = (patch == 0) | (patch == 3)

    def project(features):
        product = (jnp.dot(features, weight, preferred_element_type=F32) * LIFT).astype(F16)
        return product.reshape(2, features.shape[0] // 2, weight.shape[1])

    def slab(pair, odd):
        return lax.dynamic_index_in_dim(pair, odd ^ core, 0, keepdims=False)

    def plus(part, got):
        return (part.astype(F32) + got.astype(F32)).astype(F16)

    far, near = project(far), lax.optimization_barrier(project(near))
    outermost, inner = slab(far, 1 - patch // 2), slab(far, patch // 2)
    own, mate = slab(near, patch % 2), slab(near, 1 - patch % 2)
    first = lax.ppermute(outermost, "patch", [(0, 1), (3, 2)])
    second = jnp.where(is_end, inner, plus(outermost, first))
    up = lax.ppermute(second, "patch", [(0, 1), (1, 2)])
    down = lax.ppermute(second, "patch", [(3, 2), (2, 1)])
    third_up = plus(jnp.where(patch == 1, inner, mate), up)
    third_down = plus(jnp.where(patch == 2, inner, mate), down)
    up = lax.ppermute(third_up, "patch", [(0, 1), (1, 2), (2, 3)])
    down = lax.ppermute(third_down, "patch", [(3, 2), (2, 1), (1, 0)])
    return own, up, down


class PairGather:
    def __init__(self, own):
        self.own = own
        self.mate = lax.ppermute(own, "patch", [(0, 1), (1, 0), (2, 3), (3, 2)])
        self.across = lax.ppermute(own, "patch", [(1, 2), (2, 1)])

    def into(self, whole, index, *earlier):
        patch = lax.axis_index("patch")
        rows = self.own.shape[0]
        is_inner = (patch == 1) | (patch == 2)
        outward = [(1, 0), (2, 3)]
        across_mate = lax.ppermute(self.mate, "patch", [(1, 2), (2, 1)])
        far_inner = jnp.where(is_inner, self.across, lax.ppermute(self.across, "patch", outward))
        last = lax.ppermute(after(across_mate, *earlier), "patch", outward)
        far_outer = jnp.where(is_inner, across_mate, last)
        low = patch < 2
        slabs = (patch, patch ^ 1, jnp.where(low, 2, 1), jnp.where(low, 3, 0))
        for slab, block in zip(slabs, (self.own, self.mate, far_inner, far_outer)):
            whole = lax.dynamic_update_slice(whole, block[None], (index, slab * rows, 0))
        return whole


def sum_own_slab(features, weight, patches):
    me = lax.axis_index("patch")
    rows = features.shape[0] // patches
    parts = jnp.dot(features, weight, preferred_element_type=F32) * LIFT

    def mine(slab):
        slab = jnp.clip(slab, 0, patches - 1)
        return lax.dynamic_slice_in_dim(parts, slab * rows, rows, 0)

    up = down = None
    for step in range(1, patches):
        send_up = mine(patches - step + me)
        send_down = mine(step - patches + me)
        if step > 1:
            send_up = send_up + up.astype(F32)
            send_down = send_down + down.astype(F32)
        up = lax.ppermute(send_up.astype(F16), "patch", [(i, i + 1) for i in range(step)])
        down = lax.ppermute(
            send_down.astype(F16), "patch", [(patches - 1 - i, patches - 2 - i) for i in range(step)]
        )
    total = mine(me)
    if patches > 1:
        total = total + (up.astype(F32) + down.astype(F32))
    return (total * (1.0 / LIFT)).astype(BF16)


def attend_and_project(patches, heads, chips, chunks, place_ref, query_ref, stale_ref, key_ref, value_ref, w_ref, *out_refs):
    *out_refs, sums = out_refs
    send_refs, keep_refs = out_refs[:chunks], out_refs[chunks:]
    me = place_ref[0]
    rows = query_ref.shape[0]
    width = w_ref.shape[1] // (2 * chips)
    scale = 1.0 / HEAD_DIM**0.5
    starts = [pl.multiple_of(lax.rem(me + j, patches) * rows, rows) for j in range(1, patches)]
    dims = (((1,), (1,)), ((), ()))
    mixed_heads = []
    for h in range(heads):
        columns = slice(h * HEAD_DIM, (h + 1) * HEAD_DIM)
        query = query_ref[:, columns]
        keys = [key_ref[:, columns]] + [stale_ref[0, pl.ds(start, rows), columns] for start in starts]
        values = [value_ref[:, columns]] + [stale_ref[1, pl.ds(start, rows), columns] for start in starts]
        scores = [lax.dot_general(query, key, dims, preferred_element_type=F32) * scale for key in keys]
        top = functools.reduce(jnp.maximum, [jnp.max(s, axis=-1, keepdims=True) for s in scores])
        total = mixed = None
        for s, value in zip(scores, values):
            expo = jnp.exp(s - top)
            count = jnp.sum(expo, axis=-1, keepdims=True)
            part = jnp.dot(expo.astype(BF16), value, preferred_element_type=F32)
            total = count if total is None else total + count
            mixed = part if mixed is None else mixed + part
        mixed_heads.append((mixed / total).astype(BF16))
    heads_out = jnp.concatenate(mixed_heads, axis=1) if heads > 1 else mixed_heads[0]
    product = jnp.dot(heads_out, w_ref[...], preferred_element_type=F32)

    @pl.when(pl.program_id(0) == 0)
    def _():
        sums[...] = product

    @pl.when(pl.program_id(0) > 0)
    def _():
        sums[...] += product

    @pl.when(pl.program_id(0) == pl.num_programs(0) - 1)
    def _():
        part = width // chunks
        for c in range(chunks):
            for j in range(chips):
                theirs = pl.multiple_of(place_ref[1 + j] * width + c * part, part)
                ours = pl.multiple_of(place_ref[1 + chips + j] * width + c * part, part)
                there = slice(j * part, (j + 1) * part)
                send_refs[c][:, there] = sums[:, pl.ds(theirs, part)].astype(BF16)
                keep_refs[c][:, there] = sums[:, pl.ds(ours, part)]


def attend(query, stale_kv, key_new, value_new, w_out, patches, ranks, *earlier):
    rows, depth = query.shape
    tokens, model = stale_kv.shape[1], w_out.shape[1]
    rank = lax.axis_index("tensor").astype(jnp.int32)
    core, chip, chips = rank % 2, rank // 2, ranks // 2
    width = model // ranks
    order = [(chip + hop) % chips for hop in range(1, chips)] + [chip]
    me = lax.axis_index("patch").astype(jnp.int32)
    place = jnp.stack([me] + [2 * c + 1 - core for c in order] + [2 * c + core for c in order])
    heads = 2 if depth % (2 * HEAD_DIM) == 0 else 1
    block = heads * HEAD_DIM
    chunks = 2 if width % (2 * 128) == 0 else 1
    part = width // chunks
    results = pl.pallas_call(
        functools.partial(attend_and_project, patches, heads, chips, chunks),
        out_shape=[jax.ShapeDtypeStruct((rows, chips * part), BF16)] * chunks
        + [jax.ShapeDtypeStruct((rows, chips * part), F32)] * chunks,
        grid_spec=pltpu.PrefetchScalarGridSpec(
            num_scalar_prefetch=1,
            grid=(depth // block,),
            in_specs=[
                pl.BlockSpec((rows, block), lambda h, p: (0, h)),
                pl.BlockSpec((2, tokens, block), lambda h, p: (0, 0, h)),
                pl.BlockSpec((rows, block), lambda h, p: (0, h)),
                pl.BlockSpec((rows, block), lambda h, p: (0, h)),
                pl.BlockSpec((block, model), lambda h, p: (h, 0)),
            ],
            out_specs=[pl.BlockSpec((rows, chips * part), lambda h, p: (0, 0))] * (2 * chunks),
            scratch_shapes=[pltpu.VMEM((rows, model), F32)],
        ),
        compiler_params=pltpu.CompilerParams(vmem_limit_bytes=48 * 2**20),
        cost_estimate=pl.CostEstimate(
            flops=4 * rows * tokens * depth + 2 * rows * depth * model,
            bytes_accessed=4 * tokens * depth + 2 * depth * model + 6 * rows * chips * width,
            transcendentals=rows * tokens * (depth // HEAD_DIM),
        ),
    )(place, query, stale_kv, key_new, value_new, w_out)
    across = [(r, r ^ 1) for r in range(ranks)]
    got = [lax.ppermute(after(send, *earlier), "tensor", across) for send in results[:chunks]]
    pieces, sends = [], []
    for mine, theirs in zip(results[chunks:], got):

        def summed(j):
            return mine[:, j * part : (j + 1) * part] + theirs[:, j * part : (j + 1) * part].astype(F32)

        arrived = []
        for hop in range(1, chips):
            pairs = [(r, (r + 2 * hop) % ranks) for r in range(ranks)]
            sends.append(summed(hop - 1).astype(BF16))
            arrived.append(lax.ppermute(sends[-1], "tensor", pairs))
        total = summed(chips - 1)
        for piece in arrived:
            total = total + piece.astype(F32)
        pieces.append(total.astype(BF16))
    return jnp.concatenate(pieces, axis=1), sends


def make_shards(patches, ranks):
    def shards(hidden_in, w_query, w_key, w_value, w_out, stale_kv):
        rows = hidden_in.shape[0]
        me = lax.axis_index("patch")
        own_stale = lax.dynamic_slice_in_dim(stale_kv, me * rows, rows, 1)
        in_pairs = patches == ranks == 4
        w_both = jnp.concatenate([w_key, w_value], axis=1)
        if in_pairs:
            far, near = spread_in_pairs(hidden_in)
            both = sum_in_pairs(far, near, w_both)
            query_own, *query_got = sum_in_pairs(far, near, w_query)
        else:
            features = spread_features(hidden_in)
            both = (sum_own_slab(features, w_both, patches),)
            query = sum_own_slab(features, w_query, patches)

        def total(parts, factor):
            return functools.reduce(jnp.add, [part.astype(F32) for part in parts]) * factor

        def refresh(parts, factor, stale):
            fresh = lax.reduce_precision(total(parts, factor), 8, 7)
            stale = stale.astype(F32)
            return (stale + lax.reduce_precision(fresh - stale, 8, 7)).astype(BF16)

        width = w_key.shape[1]
        factor = 1.0 / LIFT if in_pairs else 1.0
        key_new = refresh([part[:, :width] for part in both], factor, own_stale[0])
        value_new = refresh([part[:, width:] for part in both], factor, own_stale[1])
        if in_pairs:
            *query_got, key_new, value_new = lax.optimization_barrier((*query_got, key_new, value_new))
            query = total((query_own, *query_got), factor).astype(BF16)
            keys, values = PairGather(key_new), PairGather(value_new)
            first_hop = (keys.mate, keys.across, values.mate, values.across)
        else:
            first_hop = ()
        attended, sent = attend(query, stale_kv, key_new, value_new, w_out, patches, ranks, *first_hop)
        if in_pairs:
            refreshed = keys.into(jnp.zeros_like(stale_kv), 0, *sent)
            refreshed = values.into(refreshed, 1, *sent)
        else:
            refreshed = lax.all_gather(jnp.stack([key_new, value_new]), "patch", axis=1, tiled=True)
        return (attended, refreshed)

    return shards


def solution(mesh):
    in_specs = (
        P(("groups", "patch"), "tensor"),
        P("patch", "tensor"),
        P("patch", "tensor"),
        P("patch", "tensor"),
        P("tensor", None),
        P(None, "groups", "tensor"),
    )
    out_specs = (P(("groups", "patch"), "tensor"), P(None, "groups", "tensor"))
    return jax.shard_map(
        make_shards(mesh.shape["patch"], mesh.shape["tensor"]),
        mesh=mesh,
        in_specs=in_specs,
        out_specs=out_specs,
        check_vma=False,
    )
```

```python
import functools

import jax
import jax.numpy as jnp
from jax import lax
from jax.experimental import pallas as pl
from jax.experimental.pallas import tpu as pltpu
from jax.sharding import PartitionSpec as P

HEAD_DIM = 128
F32 = jnp.float32
BF16 = jnp.bfloat16
F16 = jnp.float16
LIFT = 8.0


def spread_features(hidden):
    features = lax.all_gather(hidden, "tensor", axis=1, tiled=True)
    return lax.all_to_all(features, "patch", split_axis=1, concat_axis=0, tiled=True)


def after(value, *earlier):
    return lax.optimization_barrier((value, *earlier))[0] if earlier else value


def spread_in_pairs(hidden):
    rank, patch = lax.axis_index("tensor"), lax.axis_index("patch")
    half = hidden.shape[0] // 2
    across = [(r, r ^ 2) for r in range(4)]
    straight = hidden[:half]
    crossing = lax.ppermute(hidden[half:], "tensor", across)
    is_straight = patch // 2 == rank // 2

    def along(block, flip, far):
        pairs = [
            (4 * s + r, 4 * (r ^ flip) + 2 * (r // 2) + s % 2)
            for s in range(4)
            for r in range(4)
            if ((r ^ flip) // 2 != s // 2) == far
        ]
        return lax.ppermute(block, ("patch", "tensor"), pairs)

    def both_slabs(far):
        held = jnp.where(is_straight, along(straight, 0, far), along(crossing, 2, far))
        other = lax.ppermute(held, "tensor", across)
        low = jnp.where(is_straight, held, other)
        high = jnp.where(is_straight, other, held)
        mine = jnp.concatenate([low, high])
        theirs = lax.ppermute(mine, "tensor", [(r, r ^ 1) for r in range(4)])
        return jnp.concatenate([mine, theirs])

    return both_slabs(True), both_slabs(False)


def sum_in_pairs(far, near, weight):
    patch, core = lax.axis_index("patch"), lax.axis_index("tensor") % 2
    is_end = (patch == 0) | (patch == 3)

    def project(features):
        product = (jnp.dot(features, weight, preferred_element_type=F32) * LIFT).astype(F16)
        return product.reshape(2, features.shape[0] // 2, weight.shape[1])

    def slab(pair, odd):
        return lax.dynamic_index_in_dim(pair, odd ^ core, 0, keepdims=False)

    def plus(part, got):
        return (part.astype(F32) + got.astype(F32)).astype(F16)

    far, near = project(far), lax.optimization_barrier(project(near))
    outermost, inner = slab(far, 1 - patch // 2), slab(far, patch // 2)
    own, mate = slab(near, patch % 2), slab(near, 1 - patch % 2)
    first = lax.ppermute(outermost, "patch", [(0, 1), (3, 2)])
    second = jnp.where(is_end, inner, plus(outermost, first))
    up = lax.ppermute(second, "patch", [(0, 1), (1, 2)])
    down = lax.ppermute(second, "patch", [(3, 2), (2, 1)])
    third_up = plus(jnp.where(patch == 1, inner, mate), up)
    third_down = plus(jnp.where(patch == 2, inner, mate), down)
    up = lax.ppermute(third_up, "patch", [(0, 1), (1, 2), (2, 3)])
    down = lax.ppermute(third_down, "patch", [(3, 2), (2, 1), (1, 0)])
    return own, up, down


class PairGather:
    def __init__(self, own):
        self.own = own
        self.mate = lax.ppermute(own, "patch", [(0, 1), (1, 0), (2, 3), (3, 2)])
        self.across = lax.ppermute(own, "patch", [(1, 2), (2, 1)])

    def into(self, whole, index, *earlier):
        patch = lax.axis_index("patch")
        rows = self.own.shape[0]
        is_inner = (patch == 1) | (patch == 2)
        outward = [(1, 0), (2, 3)]
        across_mate = lax.ppermute(self.mate, "patch", [(1, 2), (2, 1)])
        far_inner = jnp.where(is_inner, self.across, lax.ppermute(self.across, "patch", outward))
        last = lax.ppermute(after(across_mate, *earlier), "patch", outward)
        far_outer = jnp.where(is_inner, across_mate, last)
        low = patch < 2
        slabs = (patch, patch ^ 1, jnp.where(low, 2, 1), jnp.where(low, 3, 0))
        for slab, block in zip(slabs, (self.own, self.mate, far_inner, far_outer)):
            whole = lax.dynamic_update_slice(whole, block[None], (index, slab * rows, 0))
        return whole


def sum_own_slab(features, weight, patches):
    me = lax.axis_index("patch")
    rows = features.shape[0] // patches
    parts = jnp.dot(features, weight, preferred_element_type=F32) * LIFT

    def mine(slab):
        slab = jnp.clip(slab, 0, patches - 1)
        return lax.dynamic_slice_in_dim(parts, slab * rows, rows, 0)

    up = down = None
    for step in range(1, patches):
        send_up = mine(patches - step + me)
        send_down = mine(step - patches + me)
        if step > 1:
            send_up = send_up + up.astype(F32)
            send_down = send_down + down.astype(F32)
        up = lax.ppermute(send_up.astype(F16), "patch", [(i, i + 1) for i in range(step)])
        down = lax.ppermute(
            send_down.astype(F16), "patch", [(patches - 1 - i, patches - 2 - i) for i in range(step)]
        )
    total = mine(me)
    if patches > 1:
        total = total + (up.astype(F32) + down.astype(F32))
    return (total * (1.0 / LIFT)).astype(BF16)


def attend_and_project(patches, heads, chips, chunks, place_ref, query_ref, stale_ref, key_ref, value_ref, w_ref, *out_refs):
    *out_refs, sums = out_refs
    send_refs, keep_refs = out_refs[:chunks], out_refs[chunks:]
    me = place_ref[0]
    rows = query_ref.shape[0]
    width = w_ref.shape[1] // (2 * chips)
    scale = 1.0 / HEAD_DIM**0.5
    starts = [pl.multiple_of(lax.rem(me + j, patches) * rows, rows) for j in range(1, patches)]
    dims = (((1,), (1,)), ((), ()))
    mixed_heads = []
    for h in range(heads):
        columns = slice(h * HEAD_DIM, (h + 1) * HEAD_DIM)
        query = query_ref[:, columns]
        keys = [key_ref[:, columns]] + [stale_ref[0, pl.ds(start, rows), columns] for start in starts]
        values = [value_ref[:, columns]] + [stale_ref[1, pl.ds(start, rows), columns] for start in starts]
        scores = [lax.dot_general(query, key, dims, preferred_element_type=F32) * scale for key in keys]
        top = functools.reduce(jnp.maximum, [jnp.max(s, axis=-1, keepdims=True) for s in scores])
        total = mixed = None
        for s, value in zip(scores, values):
            expo = jnp.exp(s - top)
            count = jnp.sum(expo, axis=-1, keepdims=True)
            part = jnp.dot(expo.astype(BF16), value, preferred_element_type=F32)
            total = count if total is None else total + count
            mixed = part if mixed is None else mixed + part
        mixed_heads.append((mixed / total).astype(BF16))
    heads_out = jnp.concatenate(mixed_heads, axis=1) if heads > 1 else mixed_heads[0]
    product = jnp.dot(heads_out, w_ref[...], preferred_element_type=F32)

    @pl.when(pl.program_id(0) == 0)
    def _():
        sums[...] = product

    @pl.when(pl.program_id(0) > 0)
    def _():
        sums[...] += product

    @pl.when(pl.program_id(0) == pl.num_programs(0) - 1)
    def _():
        part = width // chunks
        for c in range(chunks):
            for j in range(chips):
                theirs = pl.multiple_of(place_ref[1 + j] * width + c * part, part)
                ours = pl.multiple_of(place_ref[1 + chips + j] * width + c * part, part)
                there = slice(j * part, (j + 1) * part)
                send_refs[c][:, there] = sums[:, pl.ds(theirs, part)].astype(BF16)
                keep_refs[c][:, there] = sums[:, pl.ds(ours, part)]


def attend(query, stale_kv, key_new, value_new, w_out, patches, ranks, *earlier):
    rows, depth = query.shape
    tokens, model = stale_kv.shape[1], w_out.shape[1]
    rank = lax.axis_index("tensor").astype(jnp.int32)
    core, chip, chips = rank % 2, rank // 2, ranks // 2
    width = model // ranks
    order = [(chip + hop) % chips for hop in range(1, chips)] + [chip]
    me = lax.axis_index("patch").astype(jnp.int32)
    place = jnp.stack([me] + [2 * c + 1 - core for c in order] + [2 * c + core for c in order])
    heads = 2 if depth % (2 * HEAD_DIM) == 0 else 1
    block = heads * HEAD_DIM
    chunks = 2 if width % (2 * 128) == 0 else 1
    part = width // chunks
    results = pl.pallas_call(
        functools.partial(attend_and_project, patches, heads, chips, chunks),
        out_shape=[jax.ShapeDtypeStruct((rows, chips * part), BF16)] * chunks
        + [jax.ShapeDtypeStruct((rows, chips * part), F32)] * chunks,
        grid_spec=pltpu.PrefetchScalarGridSpec(
            num_scalar_prefetch=1,
            grid=(depth // block,),
            in_specs=[
                pl.BlockSpec((rows, block), lambda h, p: (0, h)),
                pl.BlockSpec((2, tokens, block), lambda h, p: (0, 0, h)),
                pl.BlockSpec((rows, block), lambda h, p: (0, h)),
                pl.BlockSpec((rows, block), lambda h, p: (0, h)),
                pl.BlockSpec((block, model), lambda h, p: (h, 0)),
            ],
            out_specs=[pl.BlockSpec((rows, chips * part), lambda h, p: (0, 0))] * (2 * chunks),
            scratch_shapes=[pltpu.VMEM((rows, model), F32)],
        ),
        compiler_params=pltpu.CompilerParams(vmem_limit_bytes=60 * 2**20),
        cost_estimate=pl.CostEstimate(
            flops=4 * rows * tokens * depth + 2 * rows * depth * model,
            bytes_accessed=4 * tokens * depth + 2 * depth * model + 6 * rows * chips * width,
            transcendentals=rows * tokens * (depth // HEAD_DIM),
        ),
    )(place, query, stale_kv, key_new, value_new, w_out)
    across = [(r, r ^ 1) for r in range(ranks)]
    got = [lax.ppermute(after(send, *earlier), "tensor", across) for send in results[:chunks]]
    pieces, sends = [], []
    for mine, theirs in zip(results[chunks:], got):

        def summed(j):
            return mine[:, j * part : (j + 1) * part] + theirs[:, j * part : (j + 1) * part].astype(F32)

        arrived = []
        for hop in range(1, chips):
            pairs = [(r, (r + 2 * hop) % ranks) for r in range(ranks)]
            sends.append(summed(hop - 1).astype(BF16))
            arrived.append(lax.ppermute(sends[-1], "tensor", pairs))
        total = summed(chips - 1)
        for piece in arrived:
            total = total + piece.astype(F32)
        pieces.append(total.astype(BF16))
    return jnp.concatenate(pieces, axis=1), sends


def make_shards(patches, ranks):
    def shards(hidden_in, w_query, w_key, w_value, w_out, stale_kv):
        rows = hidden_in.shape[0]
        me = lax.axis_index("patch")
        own_stale = lax.dynamic_slice_in_dim(stale_kv, me * rows, rows, 1)
        in_pairs = patches == ranks == 4
        w_both = jnp.concatenate([w_key, w_value], axis=1)
        if in_pairs:
            far, near = spread_in_pairs(hidden_in)
            both = sum_in_pairs(far, near, w_both)
            query_own, *query_got = sum_in_pairs(far, near, w_query)
        else:
            features = spread_features(hidden_in)
            both = (sum_own_slab(features, w_both, patches),)
            query = sum_own_slab(features, w_query, patches)

        def total(parts, factor):
            return functools.reduce(jnp.add, [part.astype(F32) for part in parts]) * factor

        def refresh(parts, factor, stale):
            fresh = lax.reduce_precision(total(parts, factor), 8, 7)
            stale = stale.astype(F32)
            return (stale + lax.reduce_precision(fresh - stale, 8, 7)).astype(BF16)

        width = w_key.shape[1]
        factor = 1.0 / LIFT if in_pairs else 1.0
        key_new = refresh([part[:, :width] for part in both], factor, own_stale[0])
        value_new = refresh([part[:, width:] for part in both], factor, own_stale[1])
        if in_pairs:
            *query_got, key_new, value_new = lax.optimization_barrier((*query_got, key_new, value_new))
            query = total((query_own, *query_got), factor).astype(BF16)
            keys, values = PairGather(key_new), PairGather(value_new)
            first_hop = (keys.mate, keys.across, values.mate, values.across)
        else:
            first_hop = ()
        attended, sent = attend(query, stale_kv, key_new, value_new, w_out, patches, ranks, *first_hop)
        if in_pairs:
            refreshed = keys.into(jnp.zeros_like(stale_kv), 0, *sent)
            refreshed = values.into(refreshed, 1, *sent)
        else:
            refreshed = lax.all_gather(jnp.stack([key_new, value_new]), "patch", axis=1, tiled=True)
        return (attended, refreshed)

    return shards


def solution(mesh):
    in_specs = (
        P(("groups", "patch"), "tensor"),
        P("patch", "tensor"),
        P("patch", "tensor"),
        P("patch", "tensor"),
        P("tensor", None),
        P(None, "groups", "tensor"),
    )
    out_specs = (P(("groups", "patch"), "tensor"), P(None, "groups", "tensor"))
    return jax.shard_map(
        make_shards(mesh.shape["patch"], mesh.shape["tensor"]),
        mesh=mesh,
        in_specs=in_specs,
        out_specs=out_specs,
        check_vma=False,
    )
```

```python
import functools

import jax
import jax.numpy as jnp
from jax import lax
from jax.experimental import pallas as pl
from jax.experimental.pallas import tpu as pltpu
from jax.sharding import PartitionSpec as P

HEAD_DIM = 128
F32 = jnp.float32
BF16 = jnp.bfloat16
F16 = jnp.float16
LIFT = 8.0


def spread_features(hidden):
    features = lax.all_gather(hidden, "tensor", axis=1, tiled=True)
    return lax.all_to_all(features, "patch", split_axis=1, concat_axis=0, tiled=True)


def after(value, *earlier):
    return lax.optimization_barrier((value, *earlier))[0] if earlier else value


def spread_in_pairs(hidden):
    rank, patch = lax.axis_index("tensor"), lax.axis_index("patch")
    half = hidden.shape[0] // 2
    across = [(r, r ^ 2) for r in range(4)]
    straight = hidden[:half]
    crossing = lax.ppermute(hidden[half:], "tensor", across)
    is_straight = patch // 2 == rank // 2

    def along(block, flip, far):
        pairs = [
            (4 * s + r, 4 * (r ^ flip) + 2 * (r // 2) + s % 2)
            for s in range(4)
            for r in range(4)
            if ((r ^ flip) // 2 != s // 2) == far
        ]
        return lax.ppermute(block, ("patch", "tensor"), pairs)

    def both_slabs(far):
        held = jnp.where(is_straight, along(straight, 0, far), along(crossing, 2, far))
        other = lax.ppermute(held, "tensor", across)
        low = jnp.where(is_straight, held, other)
        high = jnp.where(is_straight, other, held)
        mine = jnp.concatenate([low, high])
        theirs = lax.ppermute(mine, "tensor", [(r, r ^ 1) for r in range(4)])
        return jnp.concatenate([mine, theirs])

    return both_slabs(True), both_slabs(False)


def sum_in_pairs(far, near, weight):
    patch, core = lax.axis_index("patch"), lax.axis_index("tensor") % 2
    is_end = (patch == 0) | (patch == 3)

    def project(features):
        product = (jnp.dot(features, weight, preferred_element_type=F32) * LIFT).astype(F16)
        return product.reshape(2, features.shape[0] // 2, weight.shape[1])

    def slab(pair, odd):
        return lax.dynamic_index_in_dim(pair, odd ^ core, 0, keepdims=False)

    def plus(part, got):
        return (part.astype(F32) + got.astype(F32)).astype(F16)

    far, near = project(far), lax.optimization_barrier(project(near))
    outermost, inner = slab(far, 1 - patch // 2), slab(far, patch // 2)
    own, mate = slab(near, patch % 2), slab(near, 1 - patch % 2)
    first = lax.ppermute(outermost, "patch", [(0, 1), (3, 2)])
    second = jnp.where(is_end, inner, plus(outermost, first))
    up = lax.ppermute(second, "patch", [(0, 1), (1, 2)])
    down = lax.ppermute(second, "patch", [(3, 2), (2, 1)])
    hop = (up, down)
    third_up = plus(jnp.where(patch == 1, inner, mate), up)
    third_down = plus(jnp.where(patch == 2, inner, mate), down)
    up = lax.ppermute(third_up, "patch", [(0, 1), (1, 2), (2, 3)])
    down = lax.ppermute(third_down, "patch", [(3, 2), (2, 1), (1, 0)])
    return (own, up, down), hop


class PairGather:
    def __init__(self, own):
        self.own = own
        self.mate = lax.ppermute(own, "patch", [(0, 1), (1, 0), (2, 3), (3, 2)])
        self.across = lax.ppermute(own, "patch", [(1, 2), (2, 1)])

    def into(self, whole, index, *earlier):
        patch = lax.axis_index("patch")
        rows = self.own.shape[0]
        is_inner = (patch == 1) | (patch == 2)
        outward = [(1, 0), (2, 3)]
        across_mate = lax.ppermute(self.mate, "patch", [(1, 2), (2, 1)])
        far_inner = jnp.where(is_inner, self.across, lax.ppermute(self.across, "patch", outward))
        last = lax.ppermute(after(across_mate, *earlier), "patch", outward)
        far_outer = jnp.where(is_inner, across_mate, last)
        low = patch < 2
        slabs = (patch, patch ^ 1, jnp.where(low, 2, 1), jnp.where(low, 3, 0))
        for slab, block in zip(slabs, (self.own, self.mate, far_inner, far_outer)):
            whole = lax.dynamic_update_slice(whole, block[None], (index, slab * rows, 0))
        return whole


def sum_own_slab(features, weight, patches):
    me = lax.axis_index("patch")
    rows = features.shape[0] // patches
    parts = jnp.dot(features, weight, preferred_element_type=F32) * LIFT

    def mine(slab):
        slab = jnp.clip(slab, 0, patches - 1)
        return lax.dynamic_slice_in_dim(parts, slab * rows, rows, 0)

    up = down = None
    for step in range(1, patches):
        send_up = mine(patches - step + me)
        send_down = mine(step - patches + me)
        if step > 1:
            send_up = send_up + up.astype(F32)
            send_down = send_down + down.astype(F32)
        up = lax.ppermute(send_up.astype(F16), "patch", [(i, i + 1) for i in range(step)])
        down = lax.ppermute(
            send_down.astype(F16), "patch", [(patches - 1 - i, patches - 2 - i) for i in range(step)]
        )
    total = mine(me)
    if patches > 1:
        total = total + (up.astype(F32) + down.astype(F32))
    return (total * (1.0 / LIFT)).astype(BF16)


def attend_and_project(patches, heads, chips, chunks, place_ref, query_ref, stale_ref, key_ref, value_ref, w_ref, *out_refs):
    *out_refs, sums = out_refs
    send_refs, keep_refs = out_refs[:chunks], out_refs[chunks:]
    me = place_ref[0]
    rows = query_ref.shape[0]
    width = w_ref.shape[1] // (2 * chips)
    scale = 1.0 / HEAD_DIM**0.5
    starts = [pl.multiple_of(lax.rem(me + j, patches) * rows, rows) for j in range(1, patches)]
    dims = (((1,), (1,)), ((), ()))
    mixed_heads = []
    for h in range(heads):
        columns = slice(h * HEAD_DIM, (h + 1) * HEAD_DIM)
        query = query_ref[:, columns]
        keys = [key_ref[:, columns]] + [stale_ref[0, pl.ds(start, rows), columns] for start in starts]
        values = [value_ref[:, columns]] + [stale_ref[1, pl.ds(start, rows), columns] for start in starts]
        scores = [lax.dot_general(query, key, dims, preferred_element_type=F32) * scale for key in keys]
        top = functools.reduce(jnp.maximum, [jnp.max(s, axis=-1, keepdims=True) for s in scores])
        total = mixed = None
        for s, value in zip(scores, values):
            expo = jnp.exp(s - top)
            count = jnp.sum(expo, axis=-1, keepdims=True)
            part = jnp.dot(expo.astype(BF16), value, preferred_element_type=F32)
            total = count if total is None else total + count
            mixed = part if mixed is None else mixed + part
        mixed_heads.append((mixed / total).astype(BF16))
    heads_out = jnp.concatenate(mixed_heads, axis=1) if heads > 1 else mixed_heads[0]
    product = jnp.dot(heads_out, w_ref[...], preferred_element_type=F32)

    @pl.when(pl.program_id(0) == 0)
    def _():
        sums[...] = product

    @pl.when(pl.program_id(0) > 0)
    def _():
        sums[...] += product

    @pl.when(pl.program_id(0) == pl.num_programs(0) - 1)
    def _():
        part = width // chunks
        for c in range(chunks):
            for j in range(chips):
                theirs = pl.multiple_of(place_ref[1 + j] * width + c * part, part)
                ours = pl.multiple_of(place_ref[1 + chips + j] * width + c * part, part)
                there = slice(j * part, (j + 1) * part)
                send_refs[c][:, there] = sums[:, pl.ds(theirs, part)].astype(BF16)
                keep_refs[c][:, there] = sums[:, pl.ds(ours, part)]


def attend(query, stale_kv, key_new, value_new, w_out, patches, ranks, *earlier):
    rows, depth = query.shape
    tokens, model = stale_kv.shape[1], w_out.shape[1]
    rank = lax.axis_index("tensor").astype(jnp.int32)
    core, chip, chips = rank % 2, rank // 2, ranks // 2
    width = model // ranks
    order = [(chip + hop) % chips for hop in range(1, chips)] + [chip]
    me = lax.axis_index("patch").astype(jnp.int32)
    place = jnp.stack([me] + [2 * c + 1 - core for c in order] + [2 * c + core for c in order])
    heads = 2 if depth % (2 * HEAD_DIM) == 0 else 1
    block = heads * HEAD_DIM
    chunks = 2 if width % (2 * 128) == 0 else 1
    part = width // chunks
    results = pl.pallas_call(
        functools.partial(attend_and_project, patches, heads, chips, chunks),
        out_shape=[jax.ShapeDtypeStruct((rows, chips * part), BF16)] * chunks
        + [jax.ShapeDtypeStruct((rows, chips * part), F32)] * chunks,
        grid_spec=pltpu.PrefetchScalarGridSpec(
            num_scalar_prefetch=1,
            grid=(depth // block,),
            in_specs=[
                pl.BlockSpec((rows, block), lambda h, p: (0, h)),
                pl.BlockSpec((2, tokens, block), lambda h, p: (0, 0, h)),
                pl.BlockSpec((rows, block), lambda h, p: (0, h)),
                pl.BlockSpec((rows, block), lambda h, p: (0, h)),
                pl.BlockSpec((block, model), lambda h, p: (h, 0)),
            ],
            out_specs=[pl.BlockSpec((rows, chips * part), lambda h, p: (0, 0))] * (2 * chunks),
            scratch_shapes=[pltpu.VMEM((rows, model), F32)],
        ),
        compiler_params=pltpu.CompilerParams(vmem_limit_bytes=48 * 2**20),
        cost_estimate=pl.CostEstimate(
            flops=4 * rows * tokens * depth + 2 * rows * depth * model,
            bytes_accessed=4 * tokens * depth + 2 * depth * model + 6 * rows * chips * width,
            transcendentals=rows * tokens * (depth // HEAD_DIM),
        ),
    )(place, query, stale_kv, key_new, value_new, w_out)
    across = [(r, r ^ 1) for r in range(ranks)]
    got = [lax.ppermute(after(send, *earlier), "tensor", across) for send in results[:chunks]]
    pieces, sends = [], []
    for mine, theirs in zip(results[chunks:], got):

        def summed(j):
            return mine[:, j * part : (j + 1) * part] + theirs[:, j * part : (j + 1) * part].astype(F32)

        arrived = []
        for hop in range(1, chips):
            pairs = [(r, (r + 2 * hop) % ranks) for r in range(ranks)]
            sends.append(summed(hop - 1).astype(BF16))
            arrived.append(lax.ppermute(sends[-1], "tensor", pairs))
        total = summed(chips - 1)
        for piece in arrived:
            total = total + piece.astype(F32)
        pieces.append(total.astype(BF16))
    return jnp.concatenate(pieces, axis=1), sends


def make_shards(patches, ranks):
    def shards(hidden_in, w_query, w_key, w_value, w_out, stale_kv):
        rows = hidden_in.shape[0]
        me = lax.axis_index("patch")
        own_stale = lax.dynamic_slice_in_dim(stale_kv, me * rows, rows, 1)
        in_pairs = patches == ranks == 4
        w_both = jnp.concatenate([w_key, w_value], axis=1)
        if in_pairs:
            far, near = spread_in_pairs(hidden_in)
            both, _ = sum_in_pairs(far, near, w_both)
            query_parts, query_hop = sum_in_pairs(far, near, w_query)
        else:
            features = spread_features(hidden_in)
            both = (sum_own_slab(features, w_both, patches),)
            query = sum_own_slab(features, w_query, patches)

        def total(parts, factor):
            return functools.reduce(jnp.add, [part.astype(F32) for part in parts]) * factor

        def refresh(parts, factor, stale):
            fresh = lax.reduce_precision(total(parts, factor), 8, 7)
            stale = stale.astype(F32)
            return (stale + lax.reduce_precision(fresh - stale, 8, 7)).astype(BF16)

        width = w_key.shape[1]
        factor = 1.0 / LIFT if in_pairs else 1.0
        key_new = refresh([part[:, :width] for part in both], factor, own_stale[0])
        value_new = refresh([part[:, width:] for part in both], factor, own_stale[1])
        if in_pairs:
            key_new, value_new, *_ = lax.optimization_barrier((key_new, value_new, *query_hop))
            query = total(query_parts, factor).astype(BF16)
            keys, values = PairGather(key_new), PairGather(value_new)
            first_hop = (keys.mate, keys.across, values.mate, values.across)
        else:
            first_hop = ()
        attended, sent = attend(query, stale_kv, key_new, value_new, w_out, patches, ranks, *first_hop)
        if in_pairs:
            refreshed = keys.into(jnp.zeros_like(stale_kv), 0, *sent)
            refreshed = values.into(refreshed, 1, *sent)
        else:
            refreshed = lax.all_gather(jnp.stack([key_new, value_new]), "patch", axis=1, tiled=True)
        return (attended, refreshed)

    return shards


def solution(mesh):
    in_specs = (
        P(("groups", "patch"), "tensor"),
        P("patch", "tensor"),
        P("patch", "tensor"),
        P("patch", "tensor"),
        P("tensor", None),
        P(None, "groups", "tensor"),
    )
    out_specs = (P(("groups", "patch"), "tensor"), P(None, "groups", "tensor"))
    return jax.shard_map(
        make_shards(mesh.shape["patch"], mesh.shape["tensor"]),
        mesh=mesh,
        in_specs=in_specs,
        out_specs=out_specs,
        check_vma=False,
    )
```

```python
import functools

import jax
import jax.numpy as jnp
from jax import lax
from jax.experimental import pallas as pl
from jax.experimental.pallas import tpu as pltpu
from jax.sharding import PartitionSpec as P

HEAD_DIM = 128
F32 = jnp.float32
BF16 = jnp.bfloat16
F16 = jnp.float16
LIFT = 8.0


def spread_features(hidden):
    features = lax.all_gather(hidden, "tensor", axis=1, tiled=True)
    return lax.all_to_all(features, "patch", split_axis=1, concat_axis=0, tiled=True)


def after(value, *earlier):
    return lax.optimization_barrier((value, *earlier))[0] if earlier else value


def spread_in_pairs(hidden):
    rank, patch = lax.axis_index("tensor"), lax.axis_index("patch")
    half = hidden.shape[0] // 2
    across = [(r, r ^ 2) for r in range(4)]
    straight = hidden[:half]
    crossing = lax.ppermute(hidden[half:], "tensor", across)
    is_straight = patch // 2 == rank // 2

    def along(block, flip, far):
        pairs = [
            (4 * s + r, 4 * (r ^ flip) + 2 * (r // 2) + s % 2)
            for s in range(4)
            for r in range(4)
            if ((r ^ flip) // 2 != s // 2) == far
        ]
        return lax.ppermute(block, ("patch", "tensor"), pairs)

    def both_slabs(far):
        held = jnp.where(is_straight, along(straight, 0, far), along(crossing, 2, far))
        other = lax.ppermute(held, "tensor", across)
        low = jnp.where(is_straight, held, other)
        high = jnp.where(is_straight, other, held)
        mine = jnp.concatenate([low, high])
        theirs = lax.ppermute(mine, "tensor", [(r, r ^ 1) for r in range(4)])
        return jnp.concatenate([mine, theirs])

    return both_slabs(True), both_slabs(False)


def sum_in_pairs(far, near, weight):
    patch, core = lax.axis_index("patch"), lax.axis_index("tensor") % 2
    is_end = (patch == 0) | (patch == 3)

    def project(features):
        product = (jnp.dot(features, weight, preferred_element_type=F32) * LIFT).astype(F16)
        return product.reshape(2, features.shape[0] // 2, weight.shape[1])

    def slab(pair, odd):
        return lax.dynamic_index_in_dim(pair, odd ^ core, 0, keepdims=False)

    def plus(part, got):
        return (part.astype(F32) + got.astype(F32)).astype(F16)

    far, near = project(far), lax.optimization_barrier(project(near))
    outermost, inner = slab(far, 1 - patch // 2), slab(far, patch // 2)
    own, mate = slab(near, patch % 2), slab(near, 1 - patch % 2)
    first = lax.ppermute(outermost, "patch", [(0, 1), (3, 2)])
    second = jnp.where(is_end, inner, plus(outermost, first))
    up = lax.ppermute(second, "patch", [(0, 1), (1, 2)])
    down = lax.ppermute(second, "patch", [(3, 2), (2, 1)])
    hop = (up, down)
    third_up = plus(jnp.where(patch == 1, inner, mate), up)
    third_down = plus(jnp.where(patch == 2, inner, mate), down)
    up = lax.ppermute(third_up, "patch", [(0, 1), (1, 2), (2, 3)])
    down = lax.ppermute(third_down, "patch", [(3, 2), (2, 1), (1, 0)])
    return (own, up, down), hop


class PairGather:
    def __init__(self, own):
        self.own = own
        self.mate = lax.ppermute(own, "patch", [(0, 1), (1, 0), (2, 3), (3, 2)])
        self.across = lax.ppermute(own, "patch", [(1, 2), (2, 1)])

    def into(self, whole, index, *earlier):
        patch = lax.axis_index("patch")
        rows = self.own.shape[0]
        is_inner = (patch == 1) | (patch == 2)
        outward = [(1, 0), (2, 3)]
        across_mate = lax.ppermute(self.mate, "patch", [(1, 2), (2, 1)])
        far_inner = jnp.where(is_inner, self.across, lax.ppermute(self.across, "patch", outward))
        last = lax.ppermute(after(across_mate, *earlier), "patch", outward)
        far_outer = jnp.where(is_inner, across_mate, last)
        low = patch < 2
        slabs = (patch, patch ^ 1, jnp.where(low, 2, 1), jnp.where(low, 3, 0))
        for slab, block in zip(slabs, (self.own, self.mate, far_inner, far_outer)):
            whole = lax.dynamic_update_slice(whole, block[None], (index, slab * rows, 0))
        return whole


def sum_own_slab(features, weight, patches):
    me = lax.axis_index("patch")
    rows = features.shape[0] // patches
    parts = jnp.dot(features, weight, preferred_element_type=F32) * LIFT

    def mine(slab):
        slab = jnp.clip(slab, 0, patches - 1)
        return lax.dynamic_slice_in_dim(parts, slab * rows, rows, 0)

    up = down = None
    for step in range(1, patches):
        send_up = mine(patches - step + me)
        send_down = mine(step - patches + me)
        if step > 1:
            send_up = send_up + up.astype(F32)
            send_down = send_down + down.astype(F32)
        up = lax.ppermute(send_up.astype(F16), "patch", [(i, i + 1) for i in range(step)])
        down = lax.ppermute(
            send_down.astype(F16), "patch", [(patches - 1 - i, patches - 2 - i) for i in range(step)]
        )
    total = mine(me)
    if patches > 1:
        total = total + (up.astype(F32) + down.astype(F32))
    return (total * (1.0 / LIFT)).astype(BF16)


def attend_and_project(patches, heads, chips, chunks, place_ref, query_ref, stale_ref, key_ref, value_ref, w_ref, *out_refs):
    *out_refs, sums = out_refs
    send_refs, keep_refs = out_refs[:chunks], out_refs[chunks:]
    me = place_ref[0]
    rows = query_ref.shape[0]
    width = w_ref.shape[1] // (2 * chips)
    scale = 1.0 / HEAD_DIM**0.5
    starts = [pl.multiple_of(lax.rem(me + j, patches) * rows, rows) for j in range(1, patches)]
    dims = (((1,), (1,)), ((), ()))
    mixed_heads = []
    for h in range(heads):
        columns = slice(h * HEAD_DIM, (h + 1) * HEAD_DIM)
        query = query_ref[:, columns]
        keys = [key_ref[:, columns]] + [stale_ref[0, pl.ds(start, rows), columns] for start in starts]
        values = [value_ref[:, columns]] + [stale_ref[1, pl.ds(start, rows), columns] for start in starts]
        scores = [lax.dot_general(query, key, dims, preferred_element_type=F32) * scale for key in keys]
        top = functools.reduce(jnp.maximum, [jnp.max(s, axis=-1, keepdims=True) for s in scores])
        total = mixed = None
        for s, value in zip(scores, values):
            expo = jnp.exp(s - top)
            count = jnp.sum(expo, axis=-1, keepdims=True)
            part = jnp.dot(expo.astype(BF16), value, preferred_element_type=F32)
            total = count if total is None else total + count
            mixed = part if mixed is None else mixed + part
        mixed_heads.append((mixed / total).astype(BF16))
    heads_out = jnp.concatenate(mixed_heads, axis=1) if heads > 1 else mixed_heads[0]
    product = jnp.dot(heads_out, w_ref[...], preferred_element_type=F32)

    @pl.when(pl.program_id(0) == 0)
    def _():
        sums[...] = product

    @pl.when(pl.program_id(0) > 0)
    def _():
        sums[...] += product

    @pl.when(pl.program_id(0) == pl.num_programs(0) - 1)
    def _():
        part = width // chunks
        for c in range(chunks):
            for j in range(chips):
                theirs = pl.multiple_of(place_ref[1 + j] * width + c * part, part)
                ours = pl.multiple_of(place_ref[1 + chips + j] * width + c * part, part)
                there = slice(j * part, (j + 1) * part)
                send_refs[c][:, there] = sums[:, pl.ds(theirs, part)].astype(BF16)
                keep_refs[c][:, there] = sums[:, pl.ds(ours, part)]


def attend(query, stale_kv, key_new, value_new, w_out, patches, ranks, *earlier):
    rows, depth = query.shape
    tokens, model = stale_kv.shape[1], w_out.shape[1]
    rank = lax.axis_index("tensor").astype(jnp.int32)
    core, chip, chips = rank % 2, rank // 2, ranks // 2
    width = model // ranks
    order = [(chip + hop) % chips for hop in range(1, chips)] + [chip]
    me = lax.axis_index("patch").astype(jnp.int32)
    place = jnp.stack([me] + [2 * c + 1 - core for c in order] + [2 * c + core for c in order])
    heads = 2 if depth % (2 * HEAD_DIM) == 0 else 1
    block = heads * HEAD_DIM
    chunks = 2 if width % (2 * 128) == 0 else 1
    part = width // chunks
    results = pl.pallas_call(
        functools.partial(attend_and_project, patches, heads, chips, chunks),
        out_shape=[jax.ShapeDtypeStruct((rows, chips * part), BF16)] * chunks
        + [jax.ShapeDtypeStruct((rows, chips * part), F32)] * chunks,
        grid_spec=pltpu.PrefetchScalarGridSpec(
            num_scalar_prefetch=1,
            grid=(depth // block,),
            in_specs=[
                pl.BlockSpec((rows, block), lambda h, p: (0, h)),
                pl.BlockSpec((2, tokens, block), lambda h, p: (0, 0, h)),
                pl.BlockSpec((rows, block), lambda h, p: (0, h)),
                pl.BlockSpec((rows, block), lambda h, p: (0, h)),
                pl.BlockSpec((block, model), lambda h, p: (h, 0)),
            ],
            out_specs=[pl.BlockSpec((rows, chips * part), lambda h, p: (0, 0))] * (2 * chunks),
            scratch_shapes=[pltpu.VMEM((rows, model), F32)],
        ),
        compiler_params=pltpu.CompilerParams(vmem_limit_bytes=60 * 2**20),
        cost_estimate=pl.CostEstimate(
            flops=4 * rows * tokens * depth + 2 * rows * depth * model,
            bytes_accessed=4 * tokens * depth + 2 * depth * model + 6 * rows * chips * width,
            transcendentals=rows * tokens * (depth // HEAD_DIM),
        ),
    )(place, query, stale_kv, key_new, value_new, w_out)
    across = [(r, r ^ 1) for r in range(ranks)]
    got = [lax.ppermute(after(send, *earlier), "tensor", across) for send in results[:chunks]]
    pieces, sends = [], []
    for mine, theirs in zip(results[chunks:], got):

        def summed(j):
            return mine[:, j * part : (j + 1) * part] + theirs[:, j * part : (j + 1) * part].astype(F32)

        arrived = []
        for hop in range(1, chips):
            pairs = [(r, (r + 2 * hop) % ranks) for r in range(ranks)]
            sends.append(summed(hop - 1).astype(BF16))
            arrived.append(lax.ppermute(sends[-1], "tensor", pairs))
        total = summed(chips - 1)
        for piece in arrived:
            total = total + piece.astype(F32)
        pieces.append(total.astype(BF16))
    return jnp.concatenate(pieces, axis=1), sends


def make_shards(patches, ranks):
    def shards(hidden_in, w_query, w_key, w_value, w_out, stale_kv):
        rows = hidden_in.shape[0]
        me = lax.axis_index("patch")
        own_stale = lax.dynamic_slice_in_dim(stale_kv, me * rows, rows, 1)
        in_pairs = patches == ranks == 4
        w_both = jnp.concatenate([w_key, w_value], axis=1)
        if in_pairs:
            far, near = spread_in_pairs(hidden_in)
            both, _ = sum_in_pairs(far, near, w_both)
            query_parts, query_hop = sum_in_pairs(far, near, w_query)
        else:
            features = spread_features(hidden_in)
            both = (sum_own_slab(features, w_both, patches),)
            query = sum_own_slab(features, w_query, patches)

        def total(parts, factor):
            return functools.reduce(jnp.add, [part.astype(F32) for part in parts]) * factor

        def refresh(parts, factor, stale):
            fresh = lax.reduce_precision(total(parts, factor), 8, 7)
            stale = stale.astype(F32)
            return (stale + lax.reduce_precision(fresh - stale, 8, 7)).astype(BF16)

        width = w_key.shape[1]
        factor = 1.0 / LIFT if in_pairs else 1.0
        key_new = refresh([part[:, :width] for part in both], factor, own_stale[0])
        value_new = refresh([part[:, width:] for part in both], factor, own_stale[1])
        if in_pairs:
            key_new, value_new, *_ = lax.optimization_barrier((key_new, value_new, *query_hop))
            query = total(query_parts, factor).astype(BF16)
            keys, values = PairGather(key_new), PairGather(value_new)
            first_hop = (keys.mate, keys.across, values.mate, values.across)
        else:
            first_hop = ()
        attended, sent = attend(query, stale_kv, key_new, value_new, w_out, patches, ranks, *first_hop)
        if in_pairs:
            refreshed = keys.into(jnp.zeros_like(stale_kv), 0, *sent[:1])
            refreshed = values.into(refreshed, 1, *sent[:1])
        else:
            refreshed = lax.all_gather(jnp.stack([key_new, value_new]), "patch", axis=1, tiled=True)
        return (attended, refreshed)

    return shards


def solution(mesh):
    in_specs = (
        P(("groups", "patch"), "tensor"),
        P("patch", "tensor"),
        P("patch", "tensor"),
        P("patch", "tensor"),
        P("tensor", None),
        P(None, "groups", "tensor"),
    )
    out_specs = (P(("groups", "patch"), "tensor"), P(None, "groups", "tensor"))
    return jax.shard_map(
        make_shards(mesh.shape["patch"], mesh.shape["tensor"]),
        mesh=mesh,
        in_specs=in_specs,
        out_specs=out_specs,
        check_vma=False,
    )
```

```python
import functools

import jax
import jax.numpy as jnp
from jax import lax
from jax.experimental import pallas as pl
from jax.experimental.pallas import tpu as pltpu
from jax.sharding import PartitionSpec as P

HEAD_DIM = 128
F32 = jnp.float32
BF16 = jnp.bfloat16
F16 = jnp.float16
LIFT = 8.0


def spread_features(hidden):
    features = lax.all_gather(hidden, "tensor", axis=1, tiled=True)
    return lax.all_to_all(features, "patch", split_axis=1, concat_axis=0, tiled=True)


def after(value, *earlier):
    return lax.optimization_barrier((value, *earlier))[0] if earlier else value


def spread_in_pairs(hidden):
    rank, patch = lax.axis_index("tensor"), lax.axis_index("patch")
    half = hidden.shape[0] // 2
    across = [(r, r ^ 2) for r in range(4)]
    straight = hidden[:half]
    crossing = lax.ppermute(hidden[half:], "tensor", across)
    is_straight = patch // 2 == rank // 2

    def along(block, flip, far):
        pairs = [
            (4 * s + r, 4 * (r ^ flip) + 2 * (r // 2) + s % 2)
            for s in range(4)
            for r in range(4)
            if ((r ^ flip) // 2 != s // 2) == far
        ]
        return lax.ppermute(block, ("patch", "tensor"), pairs)

    def both_slabs(far):
        held = jnp.where(is_straight, along(straight, 0, far), along(crossing, 2, far))
        other = lax.ppermute(held, "tensor", across)
        low = jnp.where(is_straight, held, other)
        high = jnp.where(is_straight, other, held)
        mine = jnp.concatenate([low, high])
        theirs = lax.ppermute(mine, "tensor", [(r, r ^ 1) for r in range(4)])
        return jnp.concatenate([mine, theirs])

    return both_slabs(True), both_slabs(False)


def sum_in_pairs(far, near, weight):
    patch, core = lax.axis_index("patch"), lax.axis_index("tensor") % 2
    is_end = (patch == 0) | (patch == 3)

    def project(features):
        product = (jnp.dot(features, weight, preferred_element_type=F32) * LIFT).astype(F16)
        return product.reshape(2, features.shape[0] // 2, weight.shape[1])

    def slab(pair, odd):
        return lax.dynamic_index_in_dim(pair, odd ^ core, 0, keepdims=False)

    def plus(part, got):
        return (part.astype(F32) + got.astype(F32)).astype(F16)

    far, near = project(far), lax.optimization_barrier(project(near))
    outermost, inner = slab(far, 1 - patch // 2), slab(far, patch // 2)
    own, mate = slab(near, patch % 2), slab(near, 1 - patch % 2)
    first = lax.ppermute(outermost, "patch", [(0, 1), (3, 2)])
    second = jnp.where(is_end, inner, plus(outermost, first))
    up = lax.ppermute(second, "patch", [(0, 1), (1, 2)])
    down = lax.ppermute(second, "patch", [(3, 2), (2, 1)])
    hop = (up, down)
    third_up = plus(jnp.where(patch == 1, inner, mate), up)
    third_down = plus(jnp.where(patch == 2, inner, mate), down)
    up = lax.ppermute(third_up, "patch", [(0, 1), (1, 2), (2, 3)])
    down = lax.ppermute(third_down, "patch", [(3, 2), (2, 1), (1, 0)])
    return (own, up, down), hop


class PairGather:
    def __init__(self, own):
        self.own = own
        self.mate = lax.ppermute(own, "patch", [(0, 1), (1, 0), (2, 3), (3, 2)])
        self.across = lax.ppermute(own, "patch", [(1, 2), (2, 1)])

    def into(self, whole, index, *earlier):
        patch = lax.axis_index("patch")
        rows = self.own.shape[0]
        is_inner = (patch == 1) | (patch == 2)
        outward = [(1, 0), (2, 3)]
        across_mate = lax.ppermute(self.mate, "patch", [(1, 2), (2, 1)])
        far_inner = jnp.where(is_inner, self.across, lax.ppermute(self.across, "patch", outward))
        last = lax.ppermute(after(across_mate, *earlier), "patch", outward)
        far_outer = jnp.where(is_inner, across_mate, last)
        low = patch < 2
        slabs = (patch, patch ^ 1, jnp.where(low, 2, 1), jnp.where(low, 3, 0))
        for slab, block in zip(slabs, (self.own, self.mate, far_inner, far_outer)):
            whole = lax.dynamic_update_slice(whole, block[None], (index, slab * rows, 0))
        return whole


def sum_own_slab(features, weight, patches):
    me = lax.axis_index("patch")
    rows = features.shape[0] // patches
    parts = jnp.dot(features, weight, preferred_element_type=F32) * LIFT

    def mine(slab):
        slab = jnp.clip(slab, 0, patches - 1)
        return lax.dynamic_slice_in_dim(parts, slab * rows, rows, 0)

    up = down = None
    for step in range(1, patches):
        send_up = mine(patches - step + me)
        send_down = mine(step - patches + me)
        if step > 1:
            send_up = send_up + up.astype(F32)
            send_down = send_down + down.astype(F32)
        up = lax.ppermute(send_up.astype(F16), "patch", [(i, i + 1) for i in range(step)])
        down = lax.ppermute(
            send_down.astype(F16), "patch", [(patches - 1 - i, patches - 2 - i) for i in range(step)]
        )
    total = mine(me)
    if patches > 1:
        total = total + (up.astype(F32) + down.astype(F32))
    return (total * (1.0 / LIFT)).astype(BF16)


def attend_and_project(patches, heads, chips, chunks, place_ref, query_ref, stale_ref, key_ref, value_ref, w_ref, *out_refs):
    *out_refs, sums = out_refs
    send_refs, keep_refs = out_refs[:chunks], out_refs[chunks:]
    me = place_ref[0]
    rows = query_ref.shape[0]
    width = w_ref.shape[1] // (2 * chips)
    scale = 1.0 / HEAD_DIM**0.5
    starts = [pl.multiple_of(lax.rem(me + j, patches) * rows, rows) for j in range(1, patches)]
    dims = (((1,), (1,)), ((), ()))
    mixed_heads = []
    for h in range(heads):
        columns = slice(h * HEAD_DIM, (h + 1) * HEAD_DIM)
        query = query_ref[:, columns]
        keys = [key_ref[:, columns]] + [stale_ref[0, pl.ds(start, rows), columns] for start in starts]
        values = [value_ref[:, columns]] + [stale_ref[1, pl.ds(start, rows), columns] for start in starts]
        scores = [lax.dot_general(query, key, dims, preferred_element_type=F32) * scale for key in keys]
        top = functools.reduce(jnp.maximum, [jnp.max(s, axis=-1, keepdims=True) for s in scores])
        total = mixed = None
        for s, value in zip(scores, values):
            expo = jnp.exp(s - top)
            count = jnp.sum(expo, axis=-1, keepdims=True)
            part = jnp.dot(expo.astype(BF16), value, preferred_element_type=F32)
            total = count if total is None else total + count
            mixed = part if mixed is None else mixed + part
        mixed_heads.append((mixed / total).astype(BF16))
    heads_out = jnp.concatenate(mixed_heads, axis=1) if heads > 1 else mixed_heads[0]
    product = jnp.dot(heads_out, w_ref[...], preferred_element_type=F32)

    @pl.when(pl.program_id(0) == 0)
    def _():
        sums[...] = product

    @pl.when(pl.program_id(0) > 0)
    def _():
        sums[...] += product

    @pl.when(pl.program_id(0) == pl.num_programs(0) - 1)
    def _():
        part = width // chunks
        for c in range(chunks):
            for j in range(chips):
                theirs = pl.multiple_of(place_ref[1 + j] * width + c * part, part)
                ours = pl.multiple_of(place_ref[1 + chips + j] * width + c * part, part)
                there = slice(j * part, (j + 1) * part)
                send_refs[c][:, there] = sums[:, pl.ds(theirs, part)].astype(BF16)
                keep_refs[c][:, there] = sums[:, pl.ds(ours, part)]


def attend(query, stale_kv, key_new, value_new, w_out, patches, ranks, *earlier):
    rows, depth = query.shape
    tokens, model = stale_kv.shape[1], w_out.shape[1]
    rank = lax.axis_index("tensor").astype(jnp.int32)
    core, chip, chips = rank % 2, rank // 2, ranks // 2
    width = model // ranks
    order = [(chip + hop) % chips for hop in range(1, chips)] + [chip]
    me = lax.axis_index("patch").astype(jnp.int32)
    place = jnp.stack([me] + [2 * c + 1 - core for c in order] + [2 * c + core for c in order])
    heads = 2 if depth % (2 * HEAD_DIM) == 0 else 1
    block = heads * HEAD_DIM
    chunks = 1
    part = width // chunks
    results = pl.pallas_call(
        functools.partial(attend_and_project, patches, heads, chips, chunks),
        out_shape=[jax.ShapeDtypeStruct((rows, chips * part), BF16)] * chunks
        + [jax.ShapeDtypeStruct((rows, chips * part), F32)] * chunks,
        grid_spec=pltpu.PrefetchScalarGridSpec(
            num_scalar_prefetch=1,
            grid=(depth // block,),
            in_specs=[
                pl.BlockSpec((rows, block), lambda h, p: (0, h)),
                pl.BlockSpec((2, tokens, block), lambda h, p: (0, 0, h)),
                pl.BlockSpec((rows, block), lambda h, p: (0, h)),
                pl.BlockSpec((rows, block), lambda h, p: (0, h)),
                pl.BlockSpec((block, model), lambda h, p: (h, 0)),
            ],
            out_specs=[pl.BlockSpec((rows, chips * part), lambda h, p: (0, 0))] * (2 * chunks),
            scratch_shapes=[pltpu.VMEM((rows, model), F32)],
        ),
        compiler_params=pltpu.CompilerParams(vmem_limit_bytes=60 * 2**20),
        cost_estimate=pl.CostEstimate(
            flops=4 * rows * tokens * depth + 2 * rows * depth * model,
            bytes_accessed=4 * tokens * depth + 2 * depth * model + 6 * rows * chips * width,
            transcendentals=rows * tokens * (depth // HEAD_DIM),
        ),
    )(place, query, stale_kv, key_new, value_new, w_out)
    across = [(r, r ^ 1) for r in range(ranks)]
    got = [lax.ppermute(after(send, *earlier), "tensor", across) for send in results[:chunks]]
    pieces, sends = [], []
    for mine, theirs in zip(results[chunks:], got):

        def summed(j):
            return mine[:, j * part : (j + 1) * part] + theirs[:, j * part : (j + 1) * part].astype(F32)

        arrived = []
        for hop in range(1, chips):
            pairs = [(r, (r + 2 * hop) % ranks) for r in range(ranks)]
            sends.append(summed(hop - 1).astype(BF16))
            arrived.append(lax.ppermute(sends[-1], "tensor", pairs))
        total = summed(chips - 1)
        for piece in arrived:
            total = total + piece.astype(F32)
        pieces.append(total.astype(BF16))
    return jnp.concatenate(pieces, axis=1), sends


def make_shards(patches, ranks):
    def shards(hidden_in, w_query, w_key, w_value, w_out, stale_kv):
        rows = hidden_in.shape[0]
        me = lax.axis_index("patch")
        own_stale = lax.dynamic_slice_in_dim(stale_kv, me * rows, rows, 1)
        in_pairs = patches == ranks == 4
        w_both = jnp.concatenate([w_key, w_value], axis=1)
        if in_pairs:
            far, near = spread_in_pairs(hidden_in)
            both, _ = sum_in_pairs(far, near, w_both)
            query_parts, query_hop = sum_in_pairs(far, near, w_query)
        else:
            features = spread_features(hidden_in)
            both = (sum_own_slab(features, w_both, patches),)
            query = sum_own_slab(features, w_query, patches)

        def total(parts, factor):
            return functools.reduce(jnp.add, [part.astype(F32) for part in parts]) * factor

        def refresh(parts, factor, stale):
            fresh = lax.reduce_precision(total(parts, factor), 8, 7)
            stale = stale.astype(F32)
            return (stale + lax.reduce_precision(fresh - stale, 8, 7)).astype(BF16)

        width = w_key.shape[1]
        factor = 1.0 / LIFT if in_pairs else 1.0
        key_new = refresh([part[:, :width] for part in both], factor, own_stale[0])
        value_new = refresh([part[:, width:] for part in both], factor, own_stale[1])
        if in_pairs:
            key_new, value_new, *_ = lax.optimization_barrier((key_new, value_new, *query_hop))
            query = total(query_parts, factor).astype(BF16)
            keys, values = PairGather(key_new), PairGather(value_new)
            first_hop = (keys.mate, keys.across, values.mate, values.across)
        else:
            first_hop = ()
        attended, sent = attend(query, stale_kv, key_new, value_new, w_out, patches, ranks, *first_hop)
        if in_pairs:
            refreshed = keys.into(jnp.zeros_like(stale_kv), 0, *sent[:1])
            refreshed = values.into(refreshed, 1, *sent[:1])
        else:
            refreshed = lax.all_gather(jnp.stack([key_new, value_new]), "patch", axis=1, tiled=True)
        return (attended, refreshed)

    return shards


def solution(mesh):
    in_specs = (
        P(("groups", "patch"), "tensor"),
        P("patch", "tensor"),
        P("patch", "tensor"),
        P("patch", "tensor"),
        P("tensor", None),
        P(None, "groups", "tensor"),
    )
    out_specs = (P(("groups", "patch"), "tensor"), P(None, "groups", "tensor"))
    return jax.shard_map(
        make_shards(mesh.shape["patch"], mesh.shape["tensor"]),
        mesh=mesh,
        in_specs=in_specs,
        out_specs=out_specs,
        check_vma=False,
    )
```
